32 devices in a mesh: box: 4 (over y, x), dir: 8 (over z, core).
Axes of the slice: x: 2, y: 2, z: 4, core: 2. Of those that a mesh axis runs over, the one named last changes fastest.
Arguments:
- children: float32 [2, 512, 20480], P(None, 'box', 'dir'), may hold values from -6 to 6
- stencil_index: int32 [4, 81920], P(None, 'dir'), may hold values from 0 to 20479, as said below
- stencil_weights: float32 [4, 81920], P(None, 'dir'), may hold values from -0.25 to 1
- child_phase: float32 [8, 81920], P(None, 'dir'), may hold values from -3.140625 to 3.140625
- translations: float32 [2, 64, 4, 8, 2560], P(None, None, 'box'), may hold values from -0.4375 to 0.4375
- box_lengths: int32 [64], P('dir'), may hold values from 1 to 128, 3272 in all
- partner_ids: int32 [64, 128], P('dir'), may hold values from 0 to 63
- partner_kinds: int32 [64, 128], P('dir'), may hold values from 0 to 63
Outputs:
- incoming: float32 [2, 64, 4, 8, 2560], P(None, 'dir', 'box')
The draws below stay inside these ranges and needn't reach their ends.
Inputs may be any that keep to these rules, and one draw needn't show every extreme that they name: stencil_index[s, m] lies within m // 4 - 2 to m // 4 + 3 taken modulo 20480, and both ends are reached. `box_lengths`: the lengths sum to 3272.
All inputs are finite; a program needn't handle non-finite values. No bound on the sum of `box_lengths` on one device may be relied on, other than what follows from the above.
Results may differ from the reference program's by a relative error of at most 0.0003.
Values sent between devices are 32-bit elements; how exact they have to be, the bound alone decides.
A program may use at most 128 MiB of HBM per device.

```python
import math
import jax
import jax.numpy as jnp
import numpy as np
from jax import lax

KA = 20480
KB = 81920
STEN = 4
LMAX = 128
NTYPES = 64
NB_B = 64
NB_A = 512
RD = 2560
LIVE = 3272
N_BOX = 4
N_DIR = 8


def draw_stencil_index(key, part):
    centre = jnp.arange(KB, dtype=jnp.int32) // 4
    points = jnp.arange(STEN, dtype=jnp.int32)[:, None]
    jitter = jax.random.randint(key, (STEN, KB), -1, 2, dtype=jnp.int32)
    return ((centre[None, :] + points - 1 + jitter) % KA).astype(jnp.int32)


def set_ends(array, rng, smallest, high):
    index_at = [jax.random.randint(jax.random.fold_in(rng, axis), (), 0, length) for axis, length in enumerate(array.shape)]
    longest = array.shape.index(max(array.shape))
    neighbour = index_at[:longest] + [(index_at[longest] + 1) % array.shape[longest]] + index_at[longest + 1:]
    return array.at[tuple(index_at)].set(smallest).at[tuple(neighbour)].set(high)


def block_levels(stream_key, extent, pieces, least, largest):
    gain, own = 1.0, jax.random.fold_in(stream_key, 6)
    for position, blocks in pieces:
        steps = jnp.exp(jax.random.uniform(jax.random.fold_in(own, position), (blocks,), jnp.float32, least / len(pieces), largest / len(pieces)))
        gain = gain * jnp.repeat(steps, extent[position] // blocks).reshape([-1 if axis == position else 1 for axis in range(len(extent))])
    return gain


def length_profile(number_of, total, most, slope):
    loads = [(1 << 20) // math.isqrt(grade ** slope) + 1 for grade in range(2, number_of + 1)]
    spare, counts = total - most - (number_of - 1), [1] * (number_of - 1)
    while spare > 0:
        movable = [i for i in range(number_of - 1) if counts[i] < most]
        whole, remaining = sum([loads[i] for i in movable]), spare
        for i in movable:
            addition = min(most - counts[i], max(1, remaining * loads[i] // whole), spare)
            counts[i] = counts[i] + addition
            spare = spare - addition
    return np.array([most] + counts)


def ragged_sizes(rng, count, total, bound, skew):
    if count == 2:
        one = jax.random.randint(rng, (), max(1, total - bound), min(bound, total - 1) + 1)
        return jnp.stack([one, total - one])
    tallies = jnp.asarray(length_profile(count, total, bound, skew), jnp.int32)
    twos = (count - 1) // 2
    giver, sink = tallies[1:1 + 2 * twos:2], tallies[2:2 + 2 * twos:2]
    slack = jnp.minimum(giver - 1, bound - sink)
    moved = jax.random.randint(jax.random.fold_in(rng, 1), (twos,), 0, 1 << 20) % (slack + 1)
    tallies = tallies.at[1:1 + 2 * twos:2].set(giver - moved).at[2:2 + 2 * twos:2].set(sink + moved)
    return tallies[jax.random.permutation(jax.random.fold_in(rng, 2), count)]


def gaussian(key, shape, scale, reach, cuts=(), held_as=jnp.bfloat16):
    array = jax.random.normal(key, shape, jnp.float32) * scale
    if len(cuts) > 0:
        array = block_levels(key, shape, cuts, -0.22, 0.18) * array
    return jnp.clip(array, min=-reach, max=reach).astype(held_as)


def setup_inputs(seed: int = 0) -> dict:
    seeds = jax.random.split(jax.random.key(seed), 9)
    children = gaussian(seeds[0], (2, NB_A, KA), 1.0, 6.0, ((1, 4), (2, 8)), jnp.float32)
    stencil_index = draw_stencil_index(jax.random.fold_in(seeds[8], 71), 0)
    stencil_weights = jnp.clip(-0.25 + 1.25 * jax.random.uniform(seeds[2], (STEN, KB), jnp.float32) ** block_levels(seeds[2], (STEN, KB), ((1, 8),), -0.2, 0.2), -0.25, 1.0)
    child_phase = jnp.clip(jax.random.uniform(seeds[3], (8, KB), jnp.float32, -3.140625, 3.140625), -3.140625, 3.140625)
    translations = gaussian(seeds[4], (2, NTYPES, N_BOX, N_DIR, RD), 0.03, 0.4375, ((2, 4),), jnp.float32)
    box_lengths = ragged_sizes(seeds[5], NB_B, LIVE, LMAX, 2).astype(jnp.int32)
    partner_ids = set_ends(jax.random.randint(seeds[6], (NB_B, LMAX), 0, NB_B), jax.random.fold_in(seeds[6], 1), 0, NB_B - 1).astype(jnp.int32)
    partner_kinds = set_ends(jax.random.randint(seeds[7], (NB_B, LMAX), 0, NTYPES), jax.random.fold_in(seeds[7], 1), 0, NTYPES - 1).astype(jnp.int32)
    return {"children": children, "stencil_index": stencil_index, "stencil_weights": stencil_weights, "child_phase": child_phase, "translations": translations, "box_lengths": box_lengths, "partner_ids": partner_ids, "partner_kinds": partner_kinds}


def reference(children, stencil_index, stencil_weights, child_phase, translations, box_lengths, partner_ids, partner_kinds):
    cosine = jnp.cos(child_phase)
    sine = jnp.sin(child_phase)

    def aggregate(parent):
        block = lax.dynamic_slice_in_dim(children, parent * 8, 8, axis=1)
        picked = block[:, :, stencil_index]
        fine = jnp.sum(picked * stencil_weights[None, None], axis=2)
        real_part = jnp.sum(fine[0] * cosine - fine[1] * sine, axis=0)
        imag_part = jnp.sum(fine[0] * sine + fine[1] * cosine, axis=0)
        return jnp.stack([real_part, imag_part])

    outgoing = lax.map(aggregate, jnp.arange(NB_B, dtype=jnp.int32))
    outgoing = jnp.transpose(outgoing, (1, 0, 2))
    grid = outgoing.reshape(2, NB_B, N_DIR, N_BOX, RD).transpose(0, 1, 3, 2, 4).reshape(2, NB_B, KB)
    table = translations.reshape(2, NTYPES, KB)
    slots = jnp.arange(LMAX, dtype=jnp.int32)

    def translate(target):
        rows = grid[:, partner_ids[target], :]
        kinds = table[:, partner_kinds[target], :]
        live = (slots < box_lengths[target]).astype(jnp.float32)[:, None]
        real_part = jnp.sum((kinds[0] * rows[0] - kinds[1] * rows[1]) * live, axis=0)
        imag_part = jnp.sum((kinds[0] * rows[1] + kinds[1] * rows[0]) * live, axis=0)
        return jnp.stack([real_part, imag_part])

    incoming = lax.map(translate, jnp.arange(NB_B, dtype=jnp.int32))
    incoming = jnp.transpose(incoming, (1, 0, 2))
    return incoming.reshape(2, NB_B, N_BOX, N_DIR, RD)
```

```python
import functools

import jax
import jax.numpy as jnp
from jax import lax
from jax.experimental import pallas as pl
from jax.experimental.pallas import tpu as pltpu
from jax.sharding import PartitionSpec as P

LANES = 128
F32 = jnp.float32
BF16 = jnp.bfloat16
SIN_TERMS = (1.0, -1 / 6, 1 / 120, -1 / 5040, 1 / 362880, -1 / 39916800, 1 / 6227020800)
COS_TERMS = (1.0, -1 / 2, 1 / 24, -1 / 720, 1 / 40320, -1 / 3628800, 1 / 479001600)


def split(value):
    high = value.astype(BF16)
    return high, (value - high.astype(F32)).astype(BF16)


def series(terms, square):
    total = jnp.full_like(square, terms[-1])
    for term in terms[-2::-1]:
        total = total * square + term
    return total


def sine_cosine(angle):
    half = angle * 0.5
    square = half * half
    sine = half * series(SIN_TERMS, square)
    cosine = series(COS_TERMS, square)
    return 2.0 * sine * cosine, 1.0 - 2.0 * sine * sine


def shifted_tile(before, tile):
    lane = lax.broadcasted_iota(jnp.int32, tile.shape, 1)
    return jnp.where(lane < 2, pltpu.roll(before, 2, axis=1), pltpu.roll(tile, 2, axis=1))


def rows_of(ref, part, octant, parents):
    return ref[part, pl.ds(octant, parents, stride=8), :]


def prepare_columns(held_ref, left_ref, right_ref, tile, high_ref, low_ref, parents):
    tiles = held_ref.shape[0]
    edge = isinstance(tile, int)
    here = right_ref if edge and tile == tiles else held_ref.at[tile]
    before = left_ref if edge and tile == 0 else held_ref.at[tile - 1]
    column = tile * LANES if edge else pl.multiple_of(tile * LANES, LANES)
    for octant in range(8):
        for part in range(2):
            moved = shifted_tile(
                rows_of(before, part, octant, parents), rows_of(here, part, octant, parents)
            )
            high, low = split(moved)
            rows = pl.ds((octant * 2 + part) * parents, parents)
            high_ref[rows, pl.ds(column, LANES)] = high
            low_ref[rows, pl.ds(column, LANES)] = low


def block_layout(width, span):
    block = 512 if span % 512 == 0 else span
    return block, (256 if block == 512 else -(-(block // 4 + 128) // LANES) * LANES)


def band_matrix(index_ref, weight_ref, start, first, shift, block, total, high_ref, low_ref):
    lane = lax.broadcasted_iota(jnp.int32, (1, LANES), 1) // 4
    row = lax.broadcasted_iota(jnp.int32, (48, LANES), 0)
    for tile in range(block // LANES):
        column = pl.multiple_of(start + tile * LANES, LANES)
        centre = (first + start + tile * LANES) // 4 + lane
        band = jnp.zeros((48, LANES), F32)
        for point in range(index_ref.shape[0]):
            offset = index_ref[pl.ds(point, 1), pl.ds(column, LANES)] - centre + 2
            offset = jnp.where(offset < 0, offset + total, offset)
            offset = jnp.where(offset >= total, offset - total, offset) + lane
            band = band + jnp.where(row == offset, weight_ref[pl.ds(point, 1), pl.ds(column, LANES)], 0.0)
        high, low = split(band)
        rows = pl.ds(shift + tile * 32, 48)
        high_ref[rows, pl.ds(tile * LANES, LANES)] = high
        low_ref[rows, pl.ds(tile * LANES, LANES)] = low


def aggregate_block(refs, start, base, shift, first, block, total, parents, store):
    index_ref, weight_ref, phase_ref, high_ref, low_ref, band_high, band_low, fine_ref = refs
    depth = band_high.shape[0]
    band_matrix(index_ref, weight_ref, start, first, shift, block, total, band_high, band_low)
    window = pl.ds(base, depth)
    lhs = jnp.concatenate([high_ref[:, window], high_ref[:, window], low_ref[:, window]], axis=1)
    rhs = jnp.concatenate([band_high[...], band_low[...], band_high[...]], axis=0)
    fine_ref[...] = jnp.dot(lhs, rhs, preferred_element_type=F32)
    for tile in range(block // LANES):
        lanes = pl.ds(tile * LANES, LANES)
        sine, cosine = sine_cosine(phase_ref[:, pl.ds(pl.multiple_of(start + tile * LANES, LANES), LANES)])
        real = jnp.zeros((parents, LANES), F32)
        imag = jnp.zeros((parents, LANES), F32)
        for octant in range(8):
            s, c = sine[octant : octant + 1], cosine[octant : octant + 1]
            fine_real = fine_ref[pl.ds(octant * 2 * parents, parents), lanes]
            fine_imag = fine_ref[pl.ds((octant * 2 + 1) * parents, parents), lanes]
            real = real + (fine_real * c - fine_imag * s)
            imag = imag + (fine_real * s + fine_imag * c)
        store(tile, real, imag)


def aggregate_kernel(
    parents, span, total, children_ref, left_ref, right_ref, index_ref, weight_ref, phase_ref, out_ref,
    held_ref, high_ref, low_ref, band_high, band_low, fine_ref, load_sems,
):
    fine = index_ref.shape[1]
    block = fine_ref.shape[1]
    first = lax.axis_index("dir") * fine
    tiles = held_ref.shape[0]
    loads = [
        pltpu.make_async_copy(
            children_ref.at[:, :, pl.ds(tile * LANES, LANES)], held_ref.at[tile], load_sems.at[tile]
        )
        for tile in range(tiles)
    ]
    for load in loads:
        load.start()
    for load in loads:
        load.wait()

    @pl.loop(1, tiles)
    def _(tile):
        prepare_columns(held_ref, left_ref, right_ref, tile, high_ref, low_ref, parents)

    prepare_columns(held_ref, left_ref, right_ref, 0, high_ref, low_ref, parents)
    prepare_columns(held_ref, left_ref, right_ref, tiles, high_ref, low_ref, parents)
    refs = (index_ref, weight_ref, phase_ref, high_ref, low_ref, band_high, band_low, fine_ref)
    per_section = span // block

    def clear():
        band_high[...] = jnp.zeros_like(band_high)
        band_low[...] = jnp.zeros_like(band_low)

    def run(start, base, shift, section, column):
        def store(tile, real, imag):
            lanes = pl.ds(pl.multiple_of(column + tile * LANES, LANES), LANES)
            out_ref[section, 0, :, lanes] = real
            out_ref[section, 1, :, lanes] = imag

        aggregate_block(refs, start, base, shift, first, block, total, parents, store)

    if block == 512:
        clear()

        @pl.loop(0, fine // block)
        def _(i):
            run(
                pl.multiple_of(i * block, block), pl.multiple_of(i * LANES, LANES), 0,
                i // per_section, pl.multiple_of((i % per_section) * block, block),
            )
    else:
        for i in range(fine // block):
            clear()
            coarse = i * block // 4
            base = coarse // LANES * LANES
            run(i * block, base, coarse - base, i // per_section, (i % per_section) * block)


def count_pairs(ids_ref, kinds_ref, lengths_ref, kinds, sources, loose_ref, counts_ref):
    slots = ids_ref.shape[1]
    slot = lax.broadcasted_iota(jnp.int32, (1, slots), 1)
    kind = lax.broadcasted_iota(jnp.int32, (kinds, slots), 0)
    source = lax.broadcasted_iota(jnp.int32, (2 * sources, slots), 0) % sources

    @pl.loop(0, counts_ref.shape[0])
    def _(d):
        for p in range(8):
            at = pl.ds(d * 8 + p, 1)
            live = slot < lengths_ref[at, :]
            kind_hot = ((kind == kinds_ref[at, :]) & live).astype(F32).astype(BF16)
            source_hot = (source == ids_ref[at, :]).astype(F32).astype(BF16)
            pairs = lax.dot_general(
                kind_hot, source_hot, (((1,), (1,)), ((), ())), preferred_element_type=F32
            )
            for part in range(loose_ref.shape[0]):
                loose_ref[part, pl.ds(p, kinds, stride=8), :] = pairs[:, part * LANES : (part + 1) * LANES]
        for part in range(loose_ref.shape[0]):
            counts_ref[d, :, pl.ds(part * LANES, LANES)] = loose_ref[part].astype(BF16)


def load_sources(grid_ref, column, tiles, sources_ref):
    blocks, _, parents, _ = grid_ref.shape
    sources = blocks * parents
    for tile in range(tiles):
        lanes = pl.ds(pl.multiple_of(column + tile * LANES, LANES), LANES)
        for b in range(blocks):
            for part in range(2):
                high, low = split(grid_ref[b, part, :, lanes])
                columns = pl.ds(part * LANES, LANES)
                sources_ref[tile, pl.ds(b * parents, parents), columns] = high
                sources_ref[tile, pl.ds(sources + b * parents, parents), columns] = low


def translate_tile(counts_ref, sources_ref, table_ref, d, tile, column, kinds):
    summed = jnp.dot(counts_ref[d], sources_ref[tile], preferred_element_type=F32)
    lanes = pl.ds(column, LANES)
    real = jnp.zeros((8, LANES), F32)
    imag = jnp.zeros((8, LANES), F32)
    for k in range(kinds):
        table_real = table_ref[0, pl.ds(k, 1), lanes]
        table_imag = table_ref[1, pl.ds(k, 1), lanes]
        summed_real = summed[k * 8 : k * 8 + 8, :LANES]
        summed_imag = summed[k * 8 : k * 8 + 8, LANES:]
        real = real + (table_real * summed_real - table_imag * summed_imag)
        imag = imag + (table_real * summed_imag + table_imag * summed_real)
    return real, imag


def translate_kernel(
    grid_ref, table_ref, ids_ref, kinds_ref, lengths_ref, out_ref, loose_ref, counts_ref, sources_ref
):
    kinds = table_ref.shape[1]
    count_pairs(ids_ref, kinds_ref, lengths_ref, kinds, sources_ref.shape[1] // 2, loose_ref, counts_ref)
    tiles = sources_ref.shape[0]
    load_sources(grid_ref, 0, tiles, sources_ref)

    @pl.loop(0, tiles)
    def _(tile):
        column = pl.multiple_of(tile * LANES, LANES)

        @pl.loop(0, out_ref.shape[0])
        def _(d):
            real, imag = translate_tile(counts_ref, sources_ref, table_ref, d, tile, column, kinds)
            out_ref[d, 0, :, pl.ds(column, LANES)] = real
            out_ref[d, 1, :, pl.ds(column, LANES)] = imag


def on_device(
    children, stencil_index, stencil_weights, child_phase, translations, box_lengths, partner_ids, partner_kinds
):
    box_count = lax.axis_size("box")
    dir_count = lax.axis_size("dir")
    rows, coarse = children.shape[1:]
    fine = stencil_index.shape[1]
    parents = rows // 8
    span = fine // box_count
    kinds = translations.shape[1]
    sources = parents * box_count
    block, depth = block_layout(fine, span)
    forward = [(i, (i + 1) % dir_count) for i in range(dir_count)]
    backward = [(b, a) for a, b in forward]
    left = lax.ppermute(children[:, :, coarse - LANES :], "dir", forward)
    right = lax.ppermute(children[:, :, :LANES], "dir", backward)
    lengths = jnp.broadcast_to(box_lengths[:, None], partner_ids.shape)
    lists = lax.all_gather(jnp.stack([partner_ids, partner_kinds, lengths]), "dir", axis=1, tiled=True)
    outgoing = pl.pallas_call(
        functools.partial(aggregate_kernel, parents, span, coarse * dir_count),
        out_shape=jax.ShapeDtypeStruct((box_count, 2, parents, span), F32),
        in_specs=[pl.BlockSpec(memory_space=pl.ANY)] + [pl.BlockSpec(memory_space=pltpu.VMEM)] * 5,
        scratch_shapes=[
            pltpu.VMEM((coarse // LANES, 2, rows, LANES), F32),
            pltpu.VMEM((2 * rows, coarse + LANES), BF16),
            pltpu.VMEM((2 * rows, coarse + LANES), BF16),
            pltpu.VMEM((depth, block), BF16),
            pltpu.VMEM((depth, block), BF16),
            pltpu.VMEM((2 * rows, block), F32),
            pltpu.SemaphoreType.DMA((coarse // LANES,)),
        ],
        compiler_params=pltpu.CompilerParams(vmem_limit_bytes=48 << 20),
    )(children, left, right, stencil_index, stencil_weights, child_phase)
    grid = lax.all_to_all(outgoing, "box", split_axis=0, concat_axis=0, tiled=True)
    table = lax.dynamic_index_in_dim(translations[:, :, 0], lax.axis_index("dir"), axis=2, keepdims=False)
    result = pl.pallas_call(
        translate_kernel,
        out_shape=jax.ShapeDtypeStruct((dir_count, 2, 8, span), F32),
        scratch_shapes=[
            pltpu.VMEM((2 * sources // LANES, kinds * 8, LANES), F32),
            pltpu.VMEM((dir_count, kinds * 8, 2 * sources), BF16),
            pltpu.VMEM((span // LANES, 2 * sources, 2 * LANES), BF16),
        ],
        compiler_params=pltpu.CompilerParams(vmem_limit_bytes=48 << 20),
    )(grid, table, lists[0], lists[1], lists[2])
    result = lax.all_to_all(result, "dir", split_axis=0, concat_axis=0, tiled=True)
    return jnp.transpose(result, (1, 2, 0, 3))[:, :, None]


def solution(mesh):
    return jax.shard_map(
        on_device,
        mesh=mesh,
        in_specs=(
            P(None, "box", "dir"),
            P(None, "dir"),
            P(None, "dir"),
            P(None, "dir"),
            P(None, None, "box", None, None),
            P("dir"),
            P("dir", None),
            P("dir", None),
        ),
        out_specs=P(None, "dir", "box", None, None),
        check_vma=False,
    )
```

```python
import functools

import jax
import jax.numpy as jnp
from jax import lax
from jax.experimental import pallas as pl
from jax.experimental.pallas import tpu as pltpu
from jax.sharding import PartitionSpec as P

LANES = 128
F32 = jnp.float32
BF16 = jnp.bfloat16
SIN_TERMS = (1.0, -1 / 6, 1 / 120, -1 / 5040, 1 / 362880, -1 / 39916800, 1 / 6227020800)
COS_TERMS = (1.0, -1 / 2, 1 / 24, -1 / 720, 1 / 40320, -1 / 3628800, 1 / 479001600)


def split(value):
    high = value.astype(BF16)
    return high, (value - high.astype(F32)).astype(BF16)


def series(terms, square):
    total = jnp.full_like(square, terms[-1])
    for term in terms[-2::-1]:
        total = total * square + term
    return total


def sine_cosine(angle):
    half = angle * 0.5
    square = half * half
    sine = half * series(SIN_TERMS, square)
    cosine = series(COS_TERMS, square)
    return 2.0 * sine * cosine, 1.0 - 2.0 * sine * sine


def shifted_tile(before, tile):
    lane = lax.broadcasted_iota(jnp.int32, tile.shape, 1)
    return jnp.where(lane < 2, pltpu.roll(before, 2, axis=1), pltpu.roll(tile, 2, axis=1))


def rows_of(ref, part, octant, parents):
    return ref[part, pl.ds(octant, parents, stride=8), :]


def prepare_columns(held_ref, left_ref, right_ref, tile, high_ref, low_ref, parents):
    tiles = held_ref.shape[0]
    edge = isinstance(tile, int)
    here = right_ref if edge and tile == tiles else held_ref.at[tile]
    before = left_ref if edge and tile == 0 else held_ref.at[tile - 1]
    column = tile * LANES if edge else pl.multiple_of(tile * LANES, LANES)
    for octant in range(8):
        for part in range(2):
            moved = shifted_tile(
                rows_of(before, part, octant, parents), rows_of(here, part, octant, parents)
            )
            high, low = split(moved)
            rows = pl.ds((octant * 2 + part) * parents, parents)
            high_ref[rows, pl.ds(column, LANES)] = high
            low_ref[rows, pl.ds(column, LANES)] = low


def block_layout(width, span):
    block = 512 if span % 512 == 0 else span
    return block, (256 if block == 512 else -(-(block // 4 + 128) // LANES) * LANES)


def band_matrix(index_ref, weight_ref, start, first, shift, block, total, high_ref, low_ref):
    lane = lax.broadcasted_iota(jnp.int32, (1, LANES), 1) // 4
    row = lax.broadcasted_iota(jnp.int32, (48, LANES), 0)
    for tile in range(block // LANES):
        column = pl.multiple_of(start + tile * LANES, LANES)
        centre = (first + start + tile * LANES) // 4 + lane
        band = jnp.zeros((48, LANES), F32)
        for point in range(index_ref.shape[0]):
            offset = index_ref[pl.ds(point, 1), pl.ds(column, LANES)] - centre + 2
            offset = jnp.where(offset < 0, offset + total, offset)
            offset = jnp.where(offset >= total, offset - total, offset) + lane
            band = band + jnp.where(row == offset, weight_ref[pl.ds(point, 1), pl.ds(column, LANES)], 0.0)
        high, low = split(band)
        rows = pl.ds(pl.multiple_of(shift + tile * 32, 32), 48)
        high_ref[rows, pl.ds(tile * LANES, LANES)] = high
        low_ref[rows, pl.ds(tile * LANES, LANES)] = low


def aggregate_block(refs, start, base, shift, first, block, total, parents, out_ref):
    index_ref, weight_ref, phase_ref, high_ref, low_ref, band_high, band_low, fine_ref = refs
    depth = band_high.shape[0]
    band_matrix(index_ref, weight_ref, start, first, shift, block, total, band_high, band_low)
    window = pl.ds(base, depth)
    lhs = jnp.concatenate([high_ref[:, window], high_ref[:, window], low_ref[:, window]], axis=1)
    rhs = jnp.concatenate([band_high[...], band_low[...], band_high[...]], axis=0)
    fine_ref[...] = jnp.dot(lhs, rhs, preferred_element_type=F32)
    for tile in range(block // LANES):
        lanes = pl.ds(tile * LANES, LANES)
        sine, cosine = sine_cosine(phase_ref[:, pl.ds(pl.multiple_of(start + tile * LANES, LANES), LANES)])
        real = jnp.zeros((parents, LANES), F32)
        imag = jnp.zeros((parents, LANES), F32)
        for octant in range(8):
            s, c = sine[octant : octant + 1], cosine[octant : octant + 1]
            fine_real = fine_ref[pl.ds(octant * 2 * parents, parents), lanes]
            fine_imag = fine_ref[pl.ds((octant * 2 + 1) * parents, parents), lanes]
            real = real + (fine_real * c - fine_imag * s)
            imag = imag + (fine_real * s + fine_imag * c)
        out_ref[0, :, lanes] = real
        out_ref[1, :, lanes] = imag


def count_pairs(lists_ref, kinds, sources, loose_ref, counts_ref):
    slots = lists_ref.shape[3]
    slot = lax.broadcasted_iota(jnp.int32, (1, slots), 1)
    kind = lax.broadcasted_iota(jnp.int32, (kinds, slots), 0)
    source = lax.broadcasted_iota(jnp.int32, (2 * sources, slots), 0) % sources

    @pl.loop(0, counts_ref.shape[0])
    def _(d):
        for p in range(8):
            live = slot < lists_ref[d, 2, pl.ds(p, 1), :]
            kind_hot = ((kind == lists_ref[d, 1, pl.ds(p, 1), :]) & live).astype(F32).astype(BF16)
            source_hot = (source == lists_ref[d, 0, pl.ds(p, 1), :]).astype(F32).astype(BF16)
            pairs = lax.dot_general(
                kind_hot, source_hot, (((1,), (1,)), ((), ())), preferred_element_type=F32
            )
            for part in range(loose_ref.shape[0]):
                loose_ref[part, pl.ds(p, kinds, stride=8), :] = pairs[:, part * LANES : (part + 1) * LANES]
        for part in range(loose_ref.shape[0]):
            counts_ref[d, :, pl.ds(part * LANES, LANES)] = loose_ref[part].astype(BF16)


def load_sources(grid_ref, sources_ref):
    blocks, _, parents, _ = grid_ref.shape
    sources = blocks * parents
    for tile in range(sources_ref.shape[0]):
        lanes = pl.ds(tile * LANES, LANES)
        for b in range(blocks):
            for part in range(2):
                high, low = split(grid_ref[b, part, :, lanes])
                columns = pl.ds(part * LANES, LANES)
                sources_ref[tile, pl.ds(b * parents, parents), columns] = high
                sources_ref[tile, pl.ds(sources + b * parents, parents), columns] = low


def spread_table(table_ref, column, wide_ref):
    @pl.loop(0, table_ref.shape[1] // 8)
    def _(group):
        for tile in range(wide_ref.shape[0]):
            lanes = pl.ds(pl.multiple_of(column + tile * LANES, LANES), LANES)
            for part in range(2):
                for k in range(8):
                    row = table_ref[part, pl.ds(pl.multiple_of(group * 8, 8), 8), lanes][k : k + 1]
                    wide_ref[tile, part, group * 8 + k] = jnp.broadcast_to(row, (8, LANES))


def multiply_tile(summed_ref, wide_ref, tile, out_ref):
    real = jnp.zeros((8, LANES), F32)
    imag = jnp.zeros((8, LANES), F32)
    for k in range(wide_ref.shape[2]):
        table_real, table_imag = wide_ref[tile, 0, k], wide_ref[tile, 1, k]
        summed_real = summed_ref[pl.ds(k * 8, 8), pl.ds(0, LANES)]
        summed_imag = summed_ref[pl.ds(k * 8, 8), pl.ds(LANES, LANES)]
        real = real + (table_real * summed_real - table_imag * summed_imag)
        imag = imag + (table_real * summed_imag + table_imag * summed_real)
    out_ref[0, :, pl.ds(tile * LANES, LANES)] = real
    out_ref[1, :, pl.ds(tile * LANES, LANES)] = imag


def fused_kernel(
    parents, span, total, lists_in, children_ref, index_in, weight_in, phase_in, table_in, out_ref,
    held_ref, left_ref, right_ref, index_ref, weight_ref, phase_ref, table_ref, lists_ref,
    high_ref, low_ref, band_high, band_low, fine_ref, outgoing_ref, grid_ref,
    loose_ref, counts_ref, sources_ref, wide_ref, summed_even, summed_odd, result_ref,
    load_sems, input_sems, self_sems, halo_send, halo_recv, list_send, list_recv,
    box_send, box_recv, dir_send, dir_recv,
):
    tiles = held_ref.shape[0]
    chunks, boxes, _, _, block = grid_ref.shape
    dirs = lists_ref.shape[0]
    kinds = table_ref.shape[1]
    depth = band_high.shape[0]
    my_box, my_dir = lax.axis_index("box"), lax.axis_index("dir")
    first = my_dir * index_ref.shape[1]
    mesh_type = pl.DeviceIdType.MESH

    def dir_at(step):
        return (my_dir + step + dirs) % dirs

    def box_at(step):
        return (my_box + step + boxes) % boxes

    inputs = [
        pltpu.make_async_copy(source, target, input_sems.at[i])
        for i, (source, target) in enumerate(
            [
                (index_in, index_ref), (weight_in, weight_ref), (phase_in, phase_ref),
                (lists_in, lists_ref.at[my_dir]), (table_in.at[:, :, 0, my_dir], table_ref),
            ]
        )
    ]

    def load(tile):
        return pltpu.make_async_copy(
            children_ref.at[:, :, pl.ds(pl.multiple_of(tile * LANES, LANES), LANES)],
            held_ref.at[tile], load_sems.at[tile],
        )

    @pl.loop(0, tiles)
    def _(tile):
        load(tile).start()

    for copy in inputs:
        copy.start()

    barrier = pltpu.get_barrier_semaphore()

    @pl.loop(1, dirs)
    def _(step):
        pl.semaphore_signal(barrier, inc=1, device_id={"dir": dir_at(step)}, device_id_type=mesh_type)

    @pl.loop(1, boxes)
    def _(step):
        pl.semaphore_signal(barrier, inc=1, device_id={"box": box_at(step)}, device_id_type=mesh_type)

    pl.semaphore_wait(barrier, dirs + boxes - 2)

    halos = [
        pltpu.make_async_remote_copy(
            src_ref=children_ref.at[:, :, pl.ds(column, LANES)], dst_ref=target,
            send_sem=halo_send.at[i], recv_sem=halo_recv.at[i],
            device_id={"dir": dir_at(step)}, device_id_type=mesh_type,
        )
        for i, (column, target, step) in enumerate(
            [((tiles - 1) * LANES, left_ref, 1), (0, right_ref, -1)]
        )
    ]
    for copy in halos:
        copy.start()

    def list_copy(step, owner):
        return pltpu.make_async_remote_copy(
            src_ref=lists_in, dst_ref=lists_ref.at[owner],
            send_sem=list_send.at[step], recv_sem=list_recv.at[step],
            device_id={"dir": dir_at(step)}, device_id_type=mesh_type,
        )

    @pl.loop(1, dirs)
    def _(step):
        list_copy(step, my_dir).start()

    def box_copy(chunk, step, owner):
        return pltpu.make_async_remote_copy(
            src_ref=outgoing_ref.at[chunk, step], dst_ref=grid_ref.at[chunk, owner],
            send_sem=box_send.at[chunk, step], recv_sem=box_recv.at[chunk, step],
            device_id={"box": box_at(step)}, device_id_type=mesh_type,
        )

    def own_box_copy(chunk):
        return pltpu.make_async_copy(
            outgoing_ref.at[chunk, 0], grid_ref.at[chunk, my_box], self_sems.at[0, chunk]
        )

    def dir_target(chunk, owner):
        return out_ref.at[owner, :, :, pl.ds(pl.multiple_of(chunk * block, LANES), block)]

    def dir_copy(chunk, step, owner):
        return pltpu.make_async_remote_copy(
            src_ref=result_ref.at[chunk, step], dst_ref=dir_target(chunk, owner),
            send_sem=dir_send.at[chunk, step], recv_sem=dir_recv.at[chunk, step],
            device_id={"dir": dir_at(step)}, device_id_type=mesh_type,
        )

    def own_dir_copy(chunk):
        return pltpu.make_async_copy(
            result_ref.at[chunk, 0], dir_target(chunk, my_dir), self_sems.at[1, chunk]
        )

    def clear():
        band_high[...] = jnp.zeros_like(band_high)
        band_low[...] = jnp.zeros_like(band_low)

    clear()

    @pl.loop(0, tiles)
    def _(tile):
        load(tile).wait()

    @pl.loop(1, tiles)
    def _(tile):
        prepare_columns(held_ref, left_ref, right_ref, tile, high_ref, low_ref, parents)

    def edges():
        for copy in halos:
            copy.wait_recv()
        prepare_columns(held_ref, left_ref, right_ref, 0, high_ref, low_ref, parents)
        prepare_columns(held_ref, left_ref, right_ref, tiles, high_ref, low_ref, parents)

    def lists():
        inputs[3].wait()

        @pl.loop(1, dirs)
        def _(step):
            list_copy(step, dir_at(-step)).wait_recv()

        count_pairs(lists_ref, kinds, sources_ref.shape[1] // 2, loose_ref, counts_ref)
        inputs[4].wait()

    for copy in inputs[:3]:
        copy.wait()

    refs = (index_ref, weight_ref, phase_ref, high_ref, low_ref, band_high, band_low, fine_ref)

    def aggregate(chunk):
        @pl.loop(0, boxes)
        def _(turn):
            step = (turn + 1) % boxes
            start = pl.multiple_of(box_at(step) * span + chunk * block, LANES)
            coarse = start // 4
            if block == 512:
                base, shift = pl.multiple_of(coarse, LANES), 0
            else:
                clear()
                base = pl.multiple_of(coarse // LANES * LANES, LANES)
                shift = coarse % LANES
            aggregate_block(
                refs, start, base, shift, first, block, total, parents, outgoing_ref.at[chunk, step]
            )

            @pl.when(step > 0)
            def _():
                box_copy(chunk, step, my_box).start()

        own_box_copy(chunk).start()

    def translate(chunk):
        spread_table(table_ref, chunk * block, wide_ref)
        own_box_copy(chunk).wait()

        @pl.loop(1, boxes)
        def _(step):
            box_copy(chunk, step, box_at(-step)).wait_recv()

        load_sources(grid_ref.at[chunk], sources_ref)
        count = sources_ref.shape[0]
        buffers = (summed_even, summed_odd)

        def sum_tile(d, tile, buffer):
            buffer[...] = jnp.dot(counts_ref[d], sources_ref[tile], preferred_element_type=F32)

        def items(step, parity):
            for tile in range(count):
                if tile + 1 < count:
                    sum_tile(dir_at(step), tile + 1, buffers[(parity + tile + 1) % 2])
                else:
                    sum_tile(dir_at(step + 1), 0, buffers[(parity + tile + 1) % 2])
                multiply_tile(buffers[(parity + tile) % 2], wide_ref, tile, result_ref.at[chunk, step])

        def send(step):
            @pl.when(step > 0)
            def _():
                dir_copy(chunk, step, my_dir).start()

        sum_tile(dir_at(1), 0, summed_even)
        if count % 2 == 0:

            @pl.loop(0, dirs)
            def _(turn):
                step = (turn + 1) % dirs
                items(step, 0)
                send(step)

        else:

            @pl.loop(0, dirs // 2)
            def _(turn):
                for half in range(2):
                    step = (2 * turn + half + 1) % dirs
                    items(step, half)
                    send(step)

        own_dir_copy(chunk).start()

    if chunks < 3:
        edges()

    @pl.loop(0, chunks + 1)
    def _(turn):
        @pl.when(turn < chunks)
        def _():
            aggregate((turn + 1) % chunks)

        @pl.when(turn == 0)
        def _():
            if chunks >= 3:
                edges()
            lists()

        @pl.when(turn > 0)
        def _():
            translate(turn % chunks)

    for copy in halos:
        copy.wait_send()

    @pl.loop(1, dirs)
    def _(step):
        list_copy(step, my_dir).wait_send()

    @pl.loop(0, chunks)
    def _(chunk):
        own_dir_copy(chunk).wait()

        @pl.loop(1, boxes)
        def _(step):
            box_copy(chunk, step, my_box).wait_send()

        @pl.loop(1, dirs)
        def _(step):
            dir_copy(chunk, step, my_dir).wait_send()
            dir_copy(chunk, step, dir_at(-step)).wait_recv()


def on_device(
    children, stencil_index, stencil_weights, child_phase, translations, box_lengths, partner_ids, partner_kinds
):
    boxes = lax.axis_size("box")
    dirs = lax.axis_size("dir")
    rows, coarse = children.shape[1:]
    fine = stencil_index.shape[1]
    parents = rows // 8
    span = fine // boxes
    kinds = translations.shape[1]
    sources = parents * boxes
    slots = partner_ids.shape[1]
    block, depth = block_layout(fine, span)
    chunks = span // block
    lengths = jnp.broadcast_to(box_lengths[:, None], partner_ids.shape)
    lists = jnp.stack([partner_ids, partner_kinds, lengths])
    vmem, dma = pltpu.VMEM, pltpu.SemaphoreType.DMA
    result = pl.pallas_call(
        functools.partial(fused_kernel, parents, span, coarse * dirs),
        out_shape=jax.ShapeDtypeStruct((dirs, 2, 8, span), F32),
        in_specs=[pl.BlockSpec(memory_space=pl.ANY)] * 6,
        out_specs=pl.BlockSpec(memory_space=pl.ANY),
        scratch_shapes=[
            vmem((coarse // LANES, 2, rows, LANES), F32),
            vmem((2, rows, LANES), F32),
            vmem((2, rows, LANES), F32),
            vmem(stencil_index.shape, jnp.int32),
            vmem(stencil_weights.shape, F32),
            vmem(child_phase.shape, F32),
            vmem((2, kinds, span), F32),
            vmem((dirs, 3, 8, slots), jnp.int32),
            vmem((2 * rows, coarse + LANES), BF16),
            vmem((2 * rows, coarse + LANES), BF16),
            vmem((depth, block), BF16),
            vmem((depth, block), BF16),
            vmem((2 * rows, block), F32),
            vmem((chunks, boxes, 2, parents, block), F32),
            vmem((chunks, boxes, 2, parents, block), F32),
            vmem((2 * sources // LANES, kinds * 8, LANES), F32),
            vmem((dirs, kinds * 8, 2 * sources), BF16),
            vmem((block // LANES, 2 * sources, 2 * LANES), BF16),
            vmem((block // LANES, 2, kinds, 8, LANES), F32),
            vmem((kinds * 8, 2 * LANES), F32),
            vmem((kinds * 8, 2 * LANES), F32),
            vmem((chunks, dirs, 2, 8, block), F32),
            dma((coarse // LANES,)),
            dma((5,)),
            dma((2, chunks)),
            dma((2,)),
            dma((2,)),
            dma((dirs,)),
            dma((dirs,)),
            dma((chunks, boxes)),
            dma((chunks, boxes)),
            dma((chunks, dirs)),
            dma((chunks, dirs)),
        ],
        compiler_params=pltpu.CompilerParams(
            collective_id=0, has_side_effects=True, vmem_limit_bytes=56 << 20
        ),
    )(lists, children, stencil_index, stencil_weights, child_phase, translations)
    return jnp.transpose(result, (1, 2, 0, 3))[:, :, None]


def solution(mesh):
    return jax.shard_map(
        on_device,
        mesh=mesh,
        in_specs=(
            P(None, "box", "dir"),
            P(None, "dir"),
            P(None, "dir"),
            P(None, "dir"),
            P(None, None, "box", None, None),
            P("dir"),
            P("dir", None),
            P("dir", None),
        ),
        out_specs=P(None, "dir", "box", None, None),
        check_vma=False,
    )
```

```python
import functools

import jax
import jax.numpy as jnp
from jax import lax
from jax.experimental import pallas as pl
from jax.experimental.pallas import tpu as pltpu
from jax.sharding import PartitionSpec as P

LANES = 128
F32 = jnp.float32
BF16 = jnp.bfloat16
SIN_TERMS = (1.0, -1 / 6, 1 / 120, -1 / 5040, 1 / 362880, -1 / 39916800, 1 / 6227020800)
COS_TERMS = (1.0, -1 / 2, 1 / 24, -1 / 720, 1 / 40320, -1 / 3628800, 1 / 479001600)


def split(value):
    high = value.astype(BF16)
    return high, (value - high.astype(F32)).astype(BF16)


def series(terms, square):
    total = jnp.full_like(square, terms[-1])
    for term in terms[-2::-1]:
        total = total * square + term
    return total


def sine_cosine(angle):
    half = angle * 0.5
    square = half * half
    sine = half * series(SIN_TERMS, square)
    cosine = series(COS_TERMS, square)
    return 2.0 * sine * cosine, 1.0 - 2.0 * sine * sine


def shifted_tile(before, tile):
    lane = lax.broadcasted_iota(jnp.int32, tile.shape, 1)
    return jnp.where(lane < 2, pltpu.roll(before, 2, axis=1), pltpu.roll(tile, 2, axis=1))


def rows_of(ref, part, octant, parents):
    return ref[part, pl.ds(octant, parents, stride=8), :]


def prepare_columns(held_ref, left_ref, right_ref, tile, high_ref, low_ref, parents):
    tiles = held_ref.shape[0]
    edge = isinstance(tile, int)
    here = right_ref if edge and tile == tiles else held_ref.at[tile]
    before = left_ref if edge and tile == 0 else held_ref.at[tile - 1]
    column = tile * LANES if edge else pl.multiple_of(tile * LANES, LANES)
    for octant in range(8):
        for part in range(2):
            moved = shifted_tile(
                rows_of(before, part, octant, parents), rows_of(here, part, octant, parents)
            )
            high, low = split(moved)
            rows = pl.ds((octant * 2 + part) * parents, parents)
            high_ref[rows, pl.ds(column, LANES)] = high
            low_ref[rows, pl.ds(column, LANES)] = low


def block_layout(width, span):
    block = 512 if span % 512 == 0 else span
    return block, (256 if block == 512 else -(-(block // 4 + 128) // LANES) * LANES)


def band_matrix(index_ref, weight_ref, start, first, shift, block, total, high_ref, low_ref):
    lane = lax.broadcasted_iota(jnp.int32, (1, LANES), 1) // 4
    row = lax.broadcasted_iota(jnp.int32, (48, LANES), 0)
    for tile in range(block // LANES):
        column = pl.multiple_of(start + tile * LANES, LANES)
        centre = (first + start + tile * LANES) // 4 + lane
        band = jnp.zeros((48, LANES), F32)
        for point in range(index_ref.shape[0]):
            offset = index_ref[pl.ds(point, 1), pl.ds(column, LANES)] - centre + 2
            offset = jnp.where(offset < 0, offset + total, offset)
            offset = jnp.where(offset >= total, offset - total, offset) + lane
            band = band + jnp.where(row == offset, weight_ref[pl.ds(point, 1), pl.ds(column, LANES)], 0.0)
        high, low = split(band)
        rows = pl.ds(pl.multiple_of(shift + tile * 32, 32), 48)
        high_ref[rows, pl.ds(tile * LANES, LANES)] = high
        low_ref[rows, pl.ds(tile * LANES, LANES)] = low


def interpolate(high_ref, low_ref, base, band_high, band_low, fine_ref):
    window = pl.ds(base, band_high.shape[0])
    lhs = jnp.concatenate([high_ref[:, window], high_ref[:, window], low_ref[:, window]], axis=1)
    rhs = jnp.concatenate([band_high[...], band_low[...], band_high[...]], axis=0)
    fine_ref[...] = jnp.dot(lhs, rhs, preferred_element_type=F32)


def rotate(phase_ref, start, fine_ref, parents, out_ref):
    for tile in range(fine_ref.shape[1] // LANES):
        lanes = pl.ds(tile * LANES, LANES)
        sine, cosine = sine_cosine(phase_ref[:, pl.ds(pl.multiple_of(start + tile * LANES, LANES), LANES)])
        real = jnp.zeros((parents, LANES), F32)
        imag = jnp.zeros((parents, LANES), F32)
        for octant in range(8):
            s, c = sine[octant : octant + 1], cosine[octant : octant + 1]
            fine_real = fine_ref[pl.ds(octant * 2 * parents, parents), lanes]
            fine_imag = fine_ref[pl.ds((octant * 2 + 1) * parents, parents), lanes]
            real = real + (fine_real * c - fine_imag * s)
            imag = imag + (fine_real * s + fine_imag * c)
        out_ref[0, :, lanes] = real
        out_ref[1, :, lanes] = imag


def count_pairs(lists_ref, kinds, sources, loose_ref, counts_ref):
    slots = lists_ref.shape[3]
    slot = lax.broadcasted_iota(jnp.int32, (1, slots), 1)
    kind = lax.broadcasted_iota(jnp.int32, (kinds, slots), 0)
    source = lax.broadcasted_iota(jnp.int32, (2 * sources, slots), 0) % sources

    @pl.loop(0, counts_ref.shape[0])
    def _(d):
        for p in range(8):
            live = slot < lists_ref[d, 2, pl.ds(p, 1), :]
            kind_hot = ((kind == lists_ref[d, 1, pl.ds(p, 1), :]) & live).astype(F32).astype(BF16)
            source_hot = (source == lists_ref[d, 0, pl.ds(p, 1), :]).astype(F32).astype(BF16)
            pairs = lax.dot_general(
                kind_hot, source_hot, (((1,), (1,)), ((), ())), preferred_element_type=F32
            )
            for part in range(loose_ref.shape[0]):
                loose_ref[part, pl.ds(p, kinds, stride=8), :] = pairs[:, part * LANES : (part + 1) * LANES]
        for part in range(loose_ref.shape[0]):
            counts_ref[d, :, pl.ds(part * LANES, LANES)] = loose_ref[part].astype(BF16)


def load_sources(grid_ref, sources_ref):
    blocks, _, parents, _ = grid_ref.shape
    sources = blocks * parents
    for tile in range(sources_ref.shape[0]):
        lanes = pl.ds(tile * LANES, LANES)
        for b in range(blocks):
            for part in range(2):
                high, low = split(grid_ref[b, part, :, lanes])
                columns = pl.ds(part * LANES, LANES)
                sources_ref[tile, pl.ds(b * parents, parents), columns] = high
                sources_ref[tile, pl.ds(sources + b * parents, parents), columns] = low


def spread_table(table_ref, column, wide_ref):
    @pl.loop(0, table_ref.shape[1] // 8)
    def _(group):
        for tile in range(wide_ref.shape[0]):
            lanes = pl.ds(pl.multiple_of(column + tile * LANES, LANES), LANES)
            for part in range(2):
                for k in range(8):
                    row = table_ref[part, pl.ds(pl.multiple_of(group * 8, 8), 8), lanes][k : k + 1]
                    wide_ref[tile, part, group * 8 + k] = jnp.broadcast_to(row, (8, LANES))


def multiply_tile(summed_ref, wide_ref, tile, out_ref):
    real = jnp.zeros((8, LANES), F32)
    imag = jnp.zeros((8, LANES), F32)
    for k in range(wide_ref.shape[2]):
        table_real, table_imag = wide_ref[tile, 0, k], wide_ref[tile, 1, k]
        summed_real = summed_ref[pl.ds(k * 8, 8), pl.ds(0, LANES)]
        summed_imag = summed_ref[pl.ds(k * 8, 8), pl.ds(LANES, LANES)]
        real = real + (table_real * summed_real - table_imag * summed_imag)
        imag = imag + (table_real * summed_imag + table_imag * summed_real)
    out_ref[0, :, pl.ds(tile * LANES, LANES)] = real
    out_ref[1, :, pl.ds(tile * LANES, LANES)] = imag


def fused_kernel(
    parents, span, total, ids_in, kinds_in, lengths_in, children_ref, index_in, weight_in, phase_in, table_in, out_ref,
    held_ref, left_ref, right_ref, index_ref, weight_ref, phase_ref, table_ref, lists_ref, spare_ref,
    high_ref, low_ref, high_a, low_a, fine_a, high_b, low_b, fine_b, outgoing_ref, grid_ref,
    loose_ref, counts_ref, sources_ref, wide_ref, summed_even, summed_odd, result_ref, landing_ref,
    load_sems, input_sems, self_sems, halo_send, halo_recv, list_send, list_recv,
    box_send, box_recv, dir_send, dir_recv, place_sems,
):
    tiles = held_ref.shape[0]
    chunks, boxes, _, _, block = grid_ref.shape
    dirs = lists_ref.shape[0]
    kinds = table_ref.shape[1]
    my_box, my_dir = lax.axis_index("box"), lax.axis_index("dir")
    first = my_dir * index_ref.shape[1]
    mesh_type = pl.DeviceIdType.MESH

    def dir_at(step):
        return (my_dir + step + dirs) % dirs

    def box_at(step):
        return (my_box + step + boxes) % boxes

    inputs = [
        pltpu.make_async_copy(source, target, input_sems.at[i])
        for i, (source, target) in enumerate(
            [
                (index_in, index_ref), (weight_in, weight_ref), (phase_in, phase_ref),
                (ids_in, lists_ref.at[my_dir, 0]), (kinds_in, lists_ref.at[my_dir, 1]),
                (lengths_in, spare_ref), (table_in.at[:, :, 0, my_dir], table_ref),
            ]
        )
    ]

    def load(tile):
        return pltpu.make_async_copy(
            children_ref.at[:, :, pl.ds(pl.multiple_of(tile * LANES, LANES), LANES)],
            held_ref.at[tile], load_sems.at[tile],
        )

    @pl.loop(0, tiles)
    def _(tile):
        load(tile).start()

    for copy in inputs:
        copy.start()

    barrier = pltpu.get_barrier_semaphore()

    @pl.loop(1, dirs)
    def _(step):
        pl.semaphore_signal(barrier, inc=1, device_id={"dir": dir_at(step)}, device_id_type=mesh_type)

    @pl.loop(1, boxes)
    def _(step):
        pl.semaphore_signal(barrier, inc=1, device_id={"box": box_at(step)}, device_id_type=mesh_type)

    pl.semaphore_wait(barrier, dirs + boxes - 2)

    halos = [
        pltpu.make_async_remote_copy(
            src_ref=children_ref.at[:, :, pl.ds(column, LANES)], dst_ref=target,
            send_sem=halo_send.at[i], recv_sem=halo_recv.at[i],
            device_id={"dir": dir_at(step)}, device_id_type=mesh_type,
        )
        for i, (column, target, step) in enumerate(
            [((tiles - 1) * LANES, left_ref, 1), (0, right_ref, -1)]
        )
    ]
    for copy in halos:
        copy.start()

    def list_copy(step, owner):
        return pltpu.make_async_remote_copy(
            src_ref=lists_ref.at[my_dir], dst_ref=lists_ref.at[owner],
            send_sem=list_send.at[step], recv_sem=list_recv.at[step],
            device_id={"dir": dir_at(step)}, device_id_type=mesh_type,
        )

    for copy in inputs[3:6]:
        copy.wait()
    square = (8, spare_ref.shape[1])
    own = lax.broadcasted_iota(jnp.int32, square, 0) == lax.broadcasted_iota(jnp.int32, square, 1)
    lengths = jnp.sum(jnp.where(own, spare_ref[...].astype(F32), 0.0), axis=1, keepdims=True)
    lists_ref[my_dir, 2] = jnp.broadcast_to(lengths, (8, lists_ref.shape[3])).astype(jnp.int32)

    @pl.loop(1, dirs)
    def _(step):
        list_copy(step, my_dir).start()

    def box_copy(chunk, step, owner):
        return pltpu.make_async_remote_copy(
            src_ref=outgoing_ref.at[chunk, step], dst_ref=grid_ref.at[chunk, owner],
            send_sem=box_send.at[chunk, step], recv_sem=box_recv.at[chunk, step],
            device_id={"box": box_at(step)}, device_id_type=mesh_type,
        )

    def own_box_copy(chunk):
        return pltpu.make_async_copy(
            outgoing_ref.at[chunk, 0], grid_ref.at[chunk, my_box], self_sems.at[0, chunk]
        )

    def dir_target(chunk, owner):
        return landing_ref.at[owner, :, :, pl.ds(pl.multiple_of(chunk * block, LANES), block)]

    def place(chunk, step):
        lanes = pl.ds(pl.multiple_of(chunk * block, LANES), block)
        return pltpu.make_async_copy(
            dir_target(chunk, dir_at(-step)), out_ref.at[:, :, 0, dir_at(-step), lanes],
            place_sems.at[chunk, step],
        )

    def dir_copy(chunk, step, owner):
        return pltpu.make_async_remote_copy(
            src_ref=result_ref.at[chunk, step], dst_ref=dir_target(chunk, owner),
            send_sem=dir_send.at[chunk, step], recv_sem=dir_recv.at[chunk, step],
            device_id={"dir": dir_at(step)}, device_id_type=mesh_type,
        )

    def own_dir_copy(chunk):
        return pltpu.make_async_copy(
            result_ref.at[chunk, 0], dir_target(chunk, my_dir), self_sems.at[1, chunk]
        )

    def clear():
        for ref in (high_a, low_a, high_b, low_b):
            ref[...] = jnp.zeros_like(ref)

    clear()

    @pl.loop(0, tiles)
    def _(tile):
        load(tile).wait()

    @pl.loop(1, tiles)
    def _(tile):
        prepare_columns(held_ref, left_ref, right_ref, tile, high_ref, low_ref, parents)

    def edges():
        for copy in halos:
            copy.wait_recv()
        prepare_columns(held_ref, left_ref, right_ref, 0, high_ref, low_ref, parents)
        prepare_columns(held_ref, left_ref, right_ref, tiles, high_ref, low_ref, parents)

    def lists():
        @pl.loop(1, dirs)
        def _(step):
            list_copy(step, dir_at(-step)).wait_recv()

        count_pairs(lists_ref, kinds, sources_ref.shape[1] // 2, loose_ref, counts_ref)
        inputs[6].wait()

    for copy in inputs[:3]:
        copy.wait()

    def aggregate(chunk):
        @pl.loop(0, boxes // 2)
        def _(pair):
            steps = (2 * pair + 1, (2 * pair + 2) % boxes)
            if block != 512:
                clear()
            work = []
            for step, buffers in zip(steps, ((high_a, low_a, fine_a), (high_b, low_b, fine_b))):
                start = pl.multiple_of(box_at(step) * span + chunk * block, LANES)
                coarse = start // 4
                if block == 512:
                    base, shift = pl.multiple_of(coarse, LANES), 0
                else:
                    base = pl.multiple_of(coarse // LANES * LANES, LANES)
                    shift = coarse % LANES
                work.append((start, base, shift, step) + buffers)
            for start, base, shift, step, band_high, band_low, fine_ref in work:
                band_matrix(index_ref, weight_ref, start, first, shift, block, total, band_high, band_low)
            for start, base, shift, step, band_high, band_low, fine_ref in work:
                interpolate(high_ref, low_ref, base, band_high, band_low, fine_ref)
            for start, base, shift, step, band_high, band_low, fine_ref in work:
                rotate(phase_ref, start, fine_ref, parents, outgoing_ref.at[chunk, step])
            box_copy(chunk, steps[0], my_box).start()

            @pl.when(steps[1] > 0)
            def _():
                box_copy(chunk, steps[1], my_box).start()

        own_box_copy(chunk).start()

    def translate(chunk):
        spread_table(table_ref, chunk * block, wide_ref)
        own_box_copy(chunk).wait()

        @pl.loop(1, boxes)
        def _(step):
            box_copy(chunk, step, box_at(-step)).wait_recv()

        load_sources(grid_ref.at[chunk], sources_ref)
        count = sources_ref.shape[0]
        buffers = (summed_even, summed_odd)

        def sum_tile(d, tile, buffer):
            buffer[...] = jnp.dot(counts_ref[d], sources_ref[tile], preferred_element_type=F32)

        def items(step, parity):
            for tile in range(count):
                if tile + 1 < count:
                    sum_tile(dir_at(step), tile + 1, buffers[(parity + tile + 1) % 2])
                else:
                    sum_tile(dir_at(step + 1), 0, buffers[(parity + tile + 1) % 2])
                multiply_tile(buffers[(parity + tile) % 2], wide_ref, tile, result_ref.at[chunk, step])

        def send(step):
            @pl.when(step > 0)
            def _():
                dir_copy(chunk, step, my_dir).start()

        sum_tile(dir_at(1), 0, summed_even)
        if count % 2 == 0:

            @pl.loop(0, dirs)
            def _(turn):
                step = (turn + 1) % dirs
                items(step, 0)
                send(step)

        else:

            @pl.loop(0, dirs // 2)
            def _(turn):
                for half in range(2):
                    step = (2 * turn + half + 1) % dirs
                    items(step, half)
                    send(step)

        own_dir_copy(chunk).start()

    if chunks < 3:
        edges()

    @pl.loop(0, chunks + 1)
    def _(turn):
        if chunks >= 3:
            pl.when(turn == chunks - 2)(edges)

        @pl.when(turn < chunks)
        def _():
            aggregate((turn + 1) % chunks)

        @pl.when(turn == 0)
        def _():
            lists()

        @pl.when(turn > 0)
        def _():
            translate(turn % chunks)

    for copy in halos:
        copy.wait_send()

    @pl.loop(1, dirs)
    def _(step):
        list_copy(step, my_dir).wait_send()

    @pl.loop(0, chunks)
    def _(turn):
        chunk = (turn + 1) % chunks
        own_dir_copy(chunk).wait()
        place(chunk, 0).start()

        @pl.loop(1, dirs)
        def _(step):
            dir_copy(chunk, step, dir_at(-step)).wait_recv()
            place(chunk, step).start()

        @pl.loop(1, boxes)
        def _(step):
            box_copy(chunk, step, my_box).wait_send()

    @pl.loop(0, chunks)
    def _(chunk):
        @pl.loop(1, dirs)
        def _(step):
            dir_copy(chunk, step, my_dir).wait_send()

        @pl.loop(0, dirs)
        def _(step):
            place(chunk, step).wait()


def on_device(
    children, stencil_index, stencil_weights, child_phase, translations, box_lengths, partner_ids, partner_kinds
):
    boxes = lax.axis_size("box")
    dirs = lax.axis_size("dir")
    rows, coarse = children.shape[1:]
    fine = stencil_index.shape[1]
    parents = rows // 8
    span = fine // boxes
    kinds = translations.shape[1]
    sources = parents * boxes
    slots = partner_ids.shape[1]
    block, depth = block_layout(fine, span)
    chunks = span // block
    vmem, dma = pltpu.VMEM, pltpu.SemaphoreType.DMA
    return pl.pallas_call(
        functools.partial(fused_kernel, parents, span, coarse * dirs),
        out_shape=jax.ShapeDtypeStruct((2, 8, 1, dirs, span), F32),
        in_specs=[pl.BlockSpec(memory_space=pl.ANY)] * 8,
        out_specs=pl.BlockSpec(memory_space=pl.ANY),
        scratch_shapes=[
            vmem((coarse // LANES, 2, rows, LANES), F32),
            vmem((2, rows, LANES), F32),
            vmem((2, rows, LANES), F32),
            vmem(stencil_index.shape, jnp.int32),
            vmem(stencil_weights.shape, F32),
            vmem(child_phase.shape, F32),
            vmem((2, kinds, span), F32),
            vmem((dirs, 3, 8, slots), jnp.int32),
            vmem((1, box_lengths.shape[0]), jnp.int32),
            vmem((2 * rows, coarse + LANES), BF16),
            vmem((2 * rows, coarse + LANES), BF16),
            vmem((depth, block), BF16),
            vmem((depth, block), BF16),
            vmem((2 * rows, block), F32),
            vmem((depth, block), BF16),
            vmem((depth, block), BF16),
            vmem((2 * rows, block), F32),
            vmem((chunks, boxes, 2, parents, block), F32),
            vmem((chunks, boxes, 2, parents, block), F32),
            vmem((2 * sources // LANES, kinds * 8, LANES), F32),
            vmem((dirs, kinds * 8, 2 * sources), BF16),
            vmem((block // LANES, 2 * sources, 2 * LANES), BF16),
            vmem((block // LANES, 2, kinds, 8, LANES), F32),
            vmem((kinds * 8, 2 * LANES), F32),
            vmem((kinds * 8, 2 * LANES), F32),
            vmem((chunks, dirs, 2, 8, block), F32),
            vmem((dirs, 2, 8, span), F32),
            dma((coarse // LANES,)),
            dma((7,)),
            dma((2, chunks)),
            dma((2,)),
            dma((2,)),
            dma((dirs,)),
            dma((dirs,)),
            dma((chunks, boxes)),
            dma((chunks, boxes)),
            dma((chunks, dirs)),
            dma((chunks, dirs)),
            dma((chunks, dirs)),
        ],
        compiler_params=pltpu.CompilerParams(
            collective_id=0, has_side_effects=True, vmem_limit_bytes=56 << 20
        ),
    )(partner_ids, partner_kinds, box_lengths.reshape(1, -1), children, stencil_index, stencil_weights, child_phase, translations)


def solution(mesh):
    return jax.shard_map(
        on_device,
        mesh=mesh,
        in_specs=(
            P(None, "box", "dir"),
            P(None, "dir"),
            P(None, "dir"),
            P(None, "dir"),
            P(None, None, "box", None, None),
            P("dir"),
            P("dir", None),
            P("dir", None),
        ),
        out_specs=P(None, "dir", "box", None, None),
        check_vma=False,
    )
```

```python
import functools

import jax
import jax.numpy as jnp
from jax import lax
from jax.experimental import pallas as pl
from jax.experimental.pallas import tpu as pltpu
from jax.sharding import PartitionSpec as P

LANES = 128
F32 = jnp.float32
BF16 = jnp.bfloat16
SIN_TERMS = (1.0, -1 / 6, 1 / 120, -1 / 5040, 1 / 362880, -1 / 39916800, 1 / 6227020800)
COS_TERMS = (1.0, -1 / 2, 1 / 24, -1 / 720, 1 / 40320, -1 / 3628800, 1 / 479001600)


def split(value):
    high = value.astype(BF16)
    return high, (value - high.astype(F32)).astype(BF16)


def series(terms, square):
    total = jnp.full_like(square, terms[-1])
    for term in terms[-2::-1]:
        total = total * square + term
    return total


def sine_cosine(angle):
    half = angle * 0.5
    square = half * half
    sine = half * series(SIN_TERMS, square)
    cosine = series(COS_TERMS, square)
    return 2.0 * sine * cosine, 1.0 - 2.0 * sine * sine


def shifted_tile(before, tile):
    lane = lax.broadcasted_iota(jnp.int32, tile.shape, 1)
    return jnp.where(lane < 2, pltpu.roll(before, 2, axis=1), pltpu.roll(tile, 2, axis=1))


def rows_of(ref, part, octant, parents):
    return ref[part, pl.ds(octant, parents, stride=8), :]


def prepare_columns(held_ref, left_ref, right_ref, tile, high_ref, low_ref, parents):
    tiles = held_ref.shape[0]
    edge = isinstance(tile, int)
    here = right_ref if edge and tile == tiles else held_ref.at[tile]
    before = left_ref if edge and tile == 0 else held_ref.at[tile - 1]
    column = tile * LANES if edge else pl.multiple_of(tile * LANES, LANES)
    for octant in range(8):
        for part in range(2):
            moved = shifted_tile(
                rows_of(before, part, octant, parents), rows_of(here, part, octant, parents)
            )
            high, low = split(moved)
            rows = pl.ds((octant * 2 + part) * parents, parents)
            high_ref[rows, pl.ds(column, LANES)] = high
            low_ref[rows, pl.ds(column, LANES)] = low


def block_layout(width, span):
    block = 512 if span % 512 == 0 else span
    return block, (256 if block == 512 else -(-(block // 4 + 128) // LANES) * LANES)


def band_matrix(index_ref, weight_ref, start, first, shift, block, total, high_ref, low_ref):
    lane = lax.broadcasted_iota(jnp.int32, (1, LANES), 1) // 4
    row = lax.broadcasted_iota(jnp.int32, (48, LANES), 0)
    for tile in range(block // LANES):
        column = pl.multiple_of(start + tile * LANES, LANES)
        centre = (first + start + tile * LANES) // 4 + lane
        band = jnp.zeros((48, LANES), F32)
        for point in range(index_ref.shape[0]):
            offset = index_ref[pl.ds(point, 1), pl.ds(column, LANES)] - centre + 2
            offset = jnp.where(offset < 0, offset + total, offset)
            offset = jnp.where(offset >= total, offset - total, offset) + lane
            band = band + jnp.where(row == offset, weight_ref[pl.ds(point, 1), pl.ds(column, LANES)], 0.0)
        high, low = split(band)
        rows = pl.ds(pl.multiple_of(shift + tile * 32, 32), 48)
        high_ref[rows, pl.ds(tile * LANES, LANES)] = high
        low_ref[rows, pl.ds(tile * LANES, LANES)] = low


def interpolate(high_ref, low_ref, base, band_high, band_low, fine_ref):
    window = pl.ds(base, band_high.shape[0])
    lhs = jnp.concatenate([high_ref[:, window], high_ref[:, window], low_ref[:, window]], axis=1)
    rhs = jnp.concatenate([band_high[...], band_low[...], band_high[...]], axis=0)
    fine_ref[...] = jnp.dot(lhs, rhs, preferred_element_type=F32)


def rotate(phase_ref, start, fine_ref, parents, out_ref):
    for tile in range(fine_ref.shape[1] // LANES):
        lanes = pl.ds(tile * LANES, LANES)
        sine, cosine = sine_cosine(phase_ref[:, pl.ds(pl.multiple_of(start + tile * LANES, LANES), LANES)])
        real = jnp.zeros((parents, LANES), F32)
        imag = jnp.zeros((parents, LANES), F32)
        for octant in range(8):
            s, c = sine[octant : octant + 1], cosine[octant : octant + 1]
            fine_real = fine_ref[pl.ds(octant * 2 * parents, parents), lanes]
            fine_imag = fine_ref[pl.ds((octant * 2 + 1) * parents, parents), lanes]
            real = real + (fine_real * c - fine_imag * s)
            imag = imag + (fine_real * s + fine_imag * c)
        out_ref[0, :, lanes] = real
        out_ref[1, :, lanes] = imag


def count_pairs(lists_ref, kinds, sources, loose_ref, counts_ref):
    slots = lists_ref.shape[3]
    slot = lax.broadcasted_iota(jnp.int32, (1, slots), 1)
    kind = lax.broadcasted_iota(jnp.int32, (kinds, slots), 0)
    source = lax.broadcasted_iota(jnp.int32, (2 * sources, slots), 0) % sources

    @pl.loop(0, counts_ref.shape[0])
    def _(d):
        for p in range(8):
            live = slot < lists_ref[d, 2, pl.ds(p, 1), :]
            kind_hot = ((kind == lists_ref[d, 1, pl.ds(p, 1), :]) & live).astype(F32).astype(BF16)
            source_hot = (source == lists_ref[d, 0, pl.ds(p, 1), :]).astype(F32).astype(BF16)
            pairs = lax.dot_general(
                kind_hot, source_hot, (((1,), (1,)), ((), ())), preferred_element_type=F32
            )
            for part in range(loose_ref.shape[0]):
                loose_ref[part, pl.ds(p, kinds, stride=8), :] = pairs[:, part * LANES : (part + 1) * LANES]
        for part in range(loose_ref.shape[0]):
            counts_ref[d, :, pl.ds(part * LANES, LANES)] = loose_ref[part].astype(BF16)


def load_sources(grid_ref, sources_ref):
    blocks, _, parents, _ = grid_ref.shape
    sources = blocks * parents
    for tile in range(sources_ref.shape[0]):
        lanes = pl.ds(tile * LANES, LANES)
        for b in range(blocks):
            for part in range(2):
                high, low = split(grid_ref[b, part, :, lanes])
                columns = pl.ds(part * LANES, LANES)
                sources_ref[tile, pl.ds(b * parents, parents), columns] = high
                sources_ref[tile, pl.ds(sources + b * parents, parents), columns] = low


def spread_table(table_ref, column, wide_ref):
    @pl.loop(0, table_ref.shape[1] // 8)
    def _(group):
        for tile in range(wide_ref.shape[0]):
            lanes = pl.ds(pl.multiple_of(column + tile * LANES, LANES), LANES)
            for part in range(2):
                for k in range(8):
                    row = table_ref[part, pl.ds(pl.multiple_of(group * 8, 8), 8), lanes][k : k + 1]
                    wide_ref[tile, part, group * 8 + k] = jnp.broadcast_to(row, (8, LANES))


def multiply_tile(summed_ref, wide_ref, tile, out_ref):
    real = jnp.zeros((8, LANES), F32)
    imag = jnp.zeros((8, LANES), F32)
    for k in range(wide_ref.shape[2]):
        table_real, table_imag = wide_ref[tile, 0, k], wide_ref[tile, 1, k]
        summed_real = summed_ref[pl.ds(k * 8, 8), pl.ds(0, LANES)]
        summed_imag = summed_ref[pl.ds(k * 8, 8), pl.ds(LANES, LANES)]
        real = real + (table_real * summed_real - table_imag * summed_imag)
        imag = imag + (table_real * summed_imag + table_imag * summed_real)
    out_ref[0, :, pl.ds(tile * LANES, LANES)] = real
    out_ref[1, :, pl.ds(tile * LANES, LANES)] = imag


def fused_kernel(
    parents, span, total, ids_in, kinds_in, lengths_in, children_ref, index_in, weight_in, phase_in, table_in, out_ref,
    held_ref, left_ref, right_ref, index_ref, weight_ref, phase_ref, table_ref, lists_ref, spare_ref,
    high_ref, low_ref, high_a, low_a, fine_a, high_b, low_b, fine_b, outgoing_ref, grid_ref,
    loose_ref, counts_ref, sources_ref, wide_ref, summed_even, summed_odd, result_ref, landing_ref,
    load_sems, input_sems, self_sems, halo_send, halo_recv, list_send, list_recv,
    box_send, box_recv, dir_send, dir_recv, place_sems,
):
    tiles = held_ref.shape[0]
    chunks, boxes, _, _, block = grid_ref.shape
    dirs = lists_ref.shape[0]
    kinds = table_ref.shape[1]
    my_box, my_dir = lax.axis_index("box"), lax.axis_index("dir")
    first = my_dir * index_ref.shape[1]
    mesh_type = pl.DeviceIdType.MESH

    def dir_at(step):
        return (my_dir + step + dirs) % dirs

    def box_at(step):
        return (my_box + step + boxes) % boxes

    inputs = [
        pltpu.make_async_copy(source, target, input_sems.at[i])
        for i, (source, target) in enumerate(
            [
                (index_in, index_ref), (weight_in, weight_ref), (phase_in, phase_ref),
                (ids_in, lists_ref.at[my_dir, 0]), (kinds_in, lists_ref.at[my_dir, 1]),
                (lengths_in, spare_ref), (table_in.at[:, :, 0, my_dir], table_ref),
            ]
        )
    ]

    def load(tile):
        return pltpu.make_async_copy(
            children_ref.at[:, :, pl.ds(pl.multiple_of(tile * LANES, LANES), LANES)],
            held_ref.at[tile], load_sems.at[tile],
        )

    per = tiles // boxes
    early = (0, 1, 2) if chunks >= 3 else tuple(range(per))
    late = tuple(range(3, per)) if chunks >= 3 else ()

    def over_sections(offsets, act):
        @pl.loop(0, boxes)
        def _(section):
            for offset in offsets:
                act(section * per + offset)

    def prepare(tile):
        prepare_columns(held_ref, left_ref, right_ref, tile, high_ref, low_ref, parents)

    over_sections(early, lambda tile: load(tile).start())
    for copy in inputs[3:6] + inputs[:3]:
        copy.start()
    over_sections(late, lambda tile: load(tile).start())
    inputs[6].start()

    barrier = pltpu.get_barrier_semaphore()

    @pl.loop(1, dirs)
    def _(step):
        pl.semaphore_signal(barrier, inc=1, device_id={"dir": dir_at(step)}, device_id_type=mesh_type)

    @pl.loop(1, boxes)
    def _(step):
        pl.semaphore_signal(barrier, inc=1, device_id={"box": box_at(step)}, device_id_type=mesh_type)

    def clear():
        for ref in (high_a, low_a, high_b, low_b):
            ref[...] = jnp.zeros_like(ref)

    clear()
    over_sections(early, lambda tile: load(tile).wait())
    if chunks >= 3:
        over_sections((1, 2), prepare)
    else:

        @pl.loop(1, tiles)
        def _(tile):
            prepare(tile)

    pl.semaphore_wait(barrier, dirs + boxes - 2)

    halos = [
        pltpu.make_async_remote_copy(
            src_ref=children_ref.at[:, :, pl.ds(column, LANES)], dst_ref=target,
            send_sem=halo_send.at[i], recv_sem=halo_recv.at[i],
            device_id={"dir": dir_at(step)}, device_id_type=mesh_type,
        )
        for i, (column, target, step) in enumerate(
            [((tiles - 1) * LANES, left_ref, 1), (0, right_ref, -1)]
        )
    ]
    for copy in halos:
        copy.start()

    def list_copy(step, owner):
        return pltpu.make_async_remote_copy(
            src_ref=lists_ref.at[my_dir], dst_ref=lists_ref.at[owner],
            send_sem=list_send.at[step], recv_sem=list_recv.at[step],
            device_id={"dir": dir_at(step)}, device_id_type=mesh_type,
        )

    for copy in inputs[3:6]:
        copy.wait()
    square = (8, spare_ref.shape[1])
    own = lax.broadcasted_iota(jnp.int32, square, 0) == lax.broadcasted_iota(jnp.int32, square, 1)
    lengths = jnp.sum(jnp.where(own, spare_ref[...].astype(F32), 0.0), axis=1, keepdims=True)
    lists_ref[my_dir, 2] = jnp.broadcast_to(lengths, (8, lists_ref.shape[3])).astype(jnp.int32)

    @pl.loop(1, dirs)
    def _(step):
        list_copy(step, my_dir).start()

    def box_copy(chunk, step, owner):
        return pltpu.make_async_remote_copy(
            src_ref=outgoing_ref.at[chunk, step], dst_ref=grid_ref.at[chunk, owner],
            send_sem=box_send.at[chunk, step], recv_sem=box_recv.at[chunk, step],
            device_id={"box": box_at(step)}, device_id_type=mesh_type,
        )

    def own_box_copy(chunk):
        return pltpu.make_async_copy(
            outgoing_ref.at[chunk, 0], grid_ref.at[chunk, my_box], self_sems.at[0, chunk]
        )

    def dir_target(chunk, owner):
        return landing_ref.at[owner, :, :, pl.ds(pl.multiple_of(chunk * block, LANES), block)]

    def place(chunk, step):
        lanes = pl.ds(pl.multiple_of(chunk * block, LANES), block)
        return pltpu.make_async_copy(
            dir_target(chunk, dir_at(-step)), out_ref.at[:, :, 0, dir_at(-step), lanes],
            place_sems.at[chunk, step],
        )

    def dir_copy(chunk, step, owner):
        return pltpu.make_async_remote_copy(
            src_ref=result_ref.at[chunk, step], dst_ref=dir_target(chunk, owner),
            send_sem=dir_send.at[chunk, step], recv_sem=dir_recv.at[chunk, step],
            device_id={"dir": dir_at(step)}, device_id_type=mesh_type,
        )

    def own_dir_copy(chunk):
        return pltpu.make_async_copy(
            result_ref.at[chunk, 0], dir_target(chunk, my_dir), self_sems.at[1, chunk]
        )

    def rest():
        over_sections(late, lambda tile: load(tile).wait())
        over_sections(late, prepare)

        @pl.loop(1, boxes)
        def _(section):
            prepare(section * per)

    def edges():
        for copy in halos:
            copy.wait_recv()
        prepare_columns(held_ref, left_ref, right_ref, 0, high_ref, low_ref, parents)
        prepare_columns(held_ref, left_ref, right_ref, tiles, high_ref, low_ref, parents)

    def lists():
        @pl.loop(1, dirs)
        def _(step):
            list_copy(step, dir_at(-step)).wait_recv()

        count_pairs(lists_ref, kinds, sources_ref.shape[1] // 2, loose_ref, counts_ref)
        inputs[6].wait()

    for copy in inputs[:3]:
        copy.wait()

    def aggregate(chunk):
        @pl.loop(0, boxes // 2)
        def _(pair):
            steps = (2 * pair + 1, (2 * pair + 2) % boxes)
            if block != 512:
                clear()
            work = []
            for step, buffers in zip(steps, ((high_a, low_a, fine_a), (high_b, low_b, fine_b))):
                start = pl.multiple_of(box_at(step) * span + chunk * block, LANES)
                coarse = start // 4
                if block == 512:
                    base, shift = pl.multiple_of(coarse, LANES), 0
                else:
                    base = pl.multiple_of(coarse // LANES * LANES, LANES)
                    shift = coarse % LANES
                work.append((start, base, shift, step) + buffers)
            for start, base, shift, step, band_high, band_low, fine_ref in work:
                band_matrix(index_ref, weight_ref, start, first, shift, block, total, band_high, band_low)
            for start, base, shift, step, band_high, band_low, fine_ref in work:
                interpolate(high_ref, low_ref, base, band_high, band_low, fine_ref)
            for start, base, shift, step, band_high, band_low, fine_ref in work:
                rotate(phase_ref, start, fine_ref, parents, outgoing_ref.at[chunk, step])
            box_copy(chunk, steps[0], my_box).start()

            @pl.when(steps[1] > 0)
            def _():
                box_copy(chunk, steps[1], my_box).start()

        own_box_copy(chunk).start()

    def translate(chunk):
        spread_table(table_ref, chunk * block, wide_ref)
        own_box_copy(chunk).wait()

        @pl.loop(1, boxes)
        def _(step):
            box_copy(chunk, step, box_at(-step)).wait_recv()

        load_sources(grid_ref.at[chunk], sources_ref)
        count = sources_ref.shape[0]
        buffers = (summed_even, summed_odd)

        def sum_tile(d, tile, buffer):
            buffer[...] = jnp.dot(counts_ref[d], sources_ref[tile], preferred_element_type=F32)

        def step_at(turn):
            half = (turn + 1) // 2
            return (dirs // 2 + jnp.where(turn % 2 == 1, half, -half) + dirs) % dirs

        def items(step, following, parity):
            for tile in range(count):
                if tile + 1 < count:
                    sum_tile(dir_at(step), tile + 1, buffers[(parity + tile + 1) % 2])
                else:
                    sum_tile(dir_at(following), 0, buffers[(parity + tile + 1) % 2])
                multiply_tile(buffers[(parity + tile) % 2], wide_ref, tile, result_ref.at[chunk, step])

        def send(step):
            @pl.when(step > 0)
            def _():
                dir_copy(chunk, step, my_dir).start()

        sum_tile(dir_at(step_at(0)), 0, summed_even)
        if count % 2 == 0:

            @pl.loop(0, dirs)
            def _(turn):
                step = step_at(turn)
                items(step, step_at(turn + 1), 0)
                send(step)

        else:

            @pl.loop(0, dirs // 2)
            def _(turn):
                for half in range(2):
                    step = step_at(2 * turn + half)
                    items(step, step_at(2 * turn + half + 1), half)
                    send(step)

        own_dir_copy(chunk).start()

    if chunks < 3:
        edges()

    @pl.loop(0, chunks + 1)
    def _(turn):
        @pl.when(turn > 0)
        def _():
            translate(turn % chunks)

        low = jnp.where(turn == 0, 0, jnp.where(turn == 1, 1, turn + 1))
        high = jnp.where(turn == 0, 1, jnp.minimum(turn + 2, chunks))

        @pl.loop(low, high)
        def _(order):
            if chunks >= 3:
                pl.when(order == chunks - 2)(edges)
            aggregate((order + 1) % chunks)

        @pl.when(turn == 0)
        def _():
            if chunks >= 3:
                rest()
            lists()

    for copy in halos:
        copy.wait_send()

    @pl.loop(1, dirs)
    def _(step):
        list_copy(step, my_dir).wait_send()

    @pl.loop(0, chunks)
    def _(turn):
        chunk = (turn + 1) % chunks
        own_dir_copy(chunk).wait()
        place(chunk, 0).start()

        @pl.loop(1, dirs)
        def _(step):
            dir_copy(chunk, step, dir_at(-step)).wait_recv()
            place(chunk, step).start()

        @pl.loop(1, boxes)
        def _(step):
            box_copy(chunk, step, my_box).wait_send()

    @pl.loop(0, chunks)
    def _(chunk):
        @pl.loop(1, dirs)
        def _(step):
            dir_copy(chunk, step, my_dir).wait_send()

        @pl.loop(0, dirs)
        def _(step):
            place(chunk, step).wait()


def on_device(
    children, stencil_index, stencil_weights, child_phase, translations, box_lengths, partner_ids, partner_kinds
):
    boxes = lax.axis_size("box")
    dirs = lax.axis_size("dir")
    rows, coarse = children.shape[1:]
    fine = stencil_index.shape[1]
    parents = rows // 8
    span = fine // boxes
    kinds = translations.shape[1]
    sources = parents * boxes
    slots = partner_ids.shape[1]
    block, depth = block_layout(fine, span)
    chunks = span // block
    vmem, dma = pltpu.VMEM, pltpu.SemaphoreType.DMA
    return pl.pallas_call(
        functools.partial(fused_kernel, parents, span, coarse * dirs),
        out_shape=jax.ShapeDtypeStruct((2, 8, 1, dirs, span), F32),
        in_specs=[pl.BlockSpec(memory_space=pl.ANY)] * 8,
        out_specs=pl.BlockSpec(memory_space=pl.ANY),
        scratch_shapes=[
            vmem((coarse // LANES, 2, rows, LANES), F32),
            vmem((2, rows, LANES), F32),
            vmem((2, rows, LANES), F32),
            vmem(stencil_index.shape, jnp.int32),
            vmem(stencil_weights.shape, F32),
            vmem(child_phase.shape, F32),
            vmem((2, kinds, span), F32),
            vmem((dirs, 3, 8, slots), jnp.int32),
            vmem((1, box_lengths.shape[0]), jnp.int32),
            vmem((2 * rows, coarse + LANES), BF16),
            vmem((2 * rows, coarse + LANES), BF16),
            vmem((depth, block), BF16),
            vmem((depth, block), BF16),
            vmem((2 * rows, block), F32),
            vmem((depth, block), BF16),
            vmem((depth, block), BF16),
            vmem((2 * rows, block), F32),
            vmem((chunks, boxes, 2, parents, block), F32),
            vmem((chunks, boxes, 2, parents, block), F32),
            vmem((2 * sources // LANES, kinds * 8, LANES), F32),
            vmem((dirs, kinds * 8, 2 * sources), BF16),
            vmem((block // LANES, 2 * sources, 2 * LANES), BF16),
            vmem((block // LANES, 2, kinds, 8, LANES), F32),
            vmem((kinds * 8, 2 * LANES), F32),
            vmem((kinds * 8, 2 * LANES), F32),
            vmem((chunks, dirs, 2, 8, block), F32),
            vmem((dirs, 2, 8, span), F32),
            dma((coarse // LANES,)),
            dma((7,)),
            dma((2, chunks)),
            dma((2,)),
            dma((2,)),
            dma((dirs,)),
            dma((dirs,)),
            dma((chunks, boxes)),
            dma((chunks, boxes)),
            dma((chunks, dirs)),
            dma((chunks, dirs)),
            dma((chunks, dirs)),
        ],
        compiler_params=pltpu.CompilerParams(
            collective_id=0, has_side_effects=True, vmem_limit_bytes=56 << 20
        ),
    )(partner_ids, partner_kinds, box_lengths.reshape(1, -1), children, stencil_index, stencil_weights, child_phase, translations)


def solution(mesh):
    return jax.shard_map(
        on_device,
        mesh=mesh,
        in_specs=(
            P(None, "box", "dir"),
            P(None, "dir"),
            P(None, "dir"),
            P(None, "dir"),
            P(None, None, "box", None, None),
            P("dir"),
            P("dir", None),
            P("dir", None),
        ),
        out_specs=P(None, "dir", "box", None, None),
        check_vma=False,
    )
```

```python
import functools

import jax
import jax.numpy as jnp
from jax import lax
from jax.experimental import pallas as pl
from jax.experimental.pallas import tpu as pltpu
from jax.sharding import PartitionSpec as P

LANES = 128
F32 = jnp.float32
BF16 = jnp.bfloat16
SIN_TERMS = (1.0, -1 / 6, 1 / 120, -1 / 5040, 1 / 362880, -1 / 39916800, 1 / 6227020800)
COS_TERMS = (1.0, -1 / 2, 1 / 24, -1 / 720, 1 / 40320, -1 / 3628800, 1 / 479001600)


def split(value):
    high = value.astype(BF16)
    return high, (value - high.astype(F32)).astype(BF16)


def series(terms, square):
    total = jnp.full_like(square, terms[-1])
    for term in terms[-2::-1]:
        total = total * square + term
    return total


def sine_cosine(angle):
    half = angle * 0.5
    square = half * half
    sine = half * series(SIN_TERMS, square)
    cosine = series(COS_TERMS, square)
    return 2.0 * sine * cosine, 1.0 - 2.0 * sine * sine


def shifted_tile(before, tile):
    lane = lax.broadcasted_iota(jnp.int32, tile.shape, 1)
    return jnp.where(lane < 2, pltpu.roll(before, 2, axis=1), pltpu.roll(tile, 2, axis=1))


def rows_of(ref, part, octant, parents):
    return ref[part, pl.ds(octant, parents, stride=8), :]


def prepare_columns(held_ref, left_ref, right_ref, tile, high_ref, low_ref, parents):
    tiles = held_ref.shape[0]
    edge = isinstance(tile, int)
    here = right_ref if edge and tile == tiles else held_ref.at[tile]
    before = left_ref if edge and tile == 0 else held_ref.at[tile - 1]
    column = tile * LANES if edge else pl.multiple_of(tile * LANES, LANES)
    for octant in range(8):
        for part in range(2):
            moved = shifted_tile(
                rows_of(before, part, octant, parents), rows_of(here, part, octant, parents)
            )
            high, low = split(moved)
            rows = pl.ds((octant * 2 + part) * parents, parents)
            high_ref[rows, pl.ds(column, LANES)] = high
            low_ref[rows, pl.ds(column, LANES)] = low


def block_layout(width, span):
    block = 512 if span % 512 == 0 else span
    return block, (256 if block == 512 else -(-(block // 4 + 128) // LANES) * LANES)


def band_matrix(index_ref, weight_ref, start, first, shift, block, total, high_ref, low_ref):
    lane = lax.broadcasted_iota(jnp.int32, (1, LANES), 1) // 4
    row = lax.broadcasted_iota(jnp.int32, (48, LANES), 0)
    for tile in range(block // LANES):
        column = pl.multiple_of(start + tile * LANES, LANES)
        centre = (first + start + tile * LANES) // 4 + lane
        band = jnp.zeros((48, LANES), F32)
        for point in range(index_ref.shape[0]):
            offset = index_ref[pl.ds(point, 1), pl.ds(column, LANES)] - centre + 2
            offset = jnp.where(offset < 0, offset + total, offset)
            offset = jnp.where(offset >= total, offset - total, offset) + lane
            band = band + jnp.where(row == offset, weight_ref[pl.ds(point, 1), pl.ds(column, LANES)], 0.0)
        high, low = split(band)
        rows = pl.ds(pl.multiple_of(shift + tile * 32, 32), 48)
        high_ref[rows, pl.ds(tile * LANES, LANES)] = high
        low_ref[rows, pl.ds(tile * LANES, LANES)] = low


def interpolate(high_ref, low_ref, base, band_high, band_low, fine_ref):
    window = pl.ds(base, band_high.shape[0])
    lhs = jnp.concatenate([high_ref[:, window], high_ref[:, window], low_ref[:, window]], axis=1)
    rhs = jnp.concatenate([band_high[...], band_low[...], band_high[...]], axis=0)
    fine_ref[...] = jnp.dot(lhs, rhs, preferred_element_type=F32)


def rotate(phase_ref, start, fine_ref, parents, out_ref):
    for tile in range(fine_ref.shape[1] // LANES):
        lanes = pl.ds(tile * LANES, LANES)
        sine, cosine = sine_cosine(phase_ref[:, pl.ds(pl.multiple_of(start + tile * LANES, LANES), LANES)])
        real = jnp.zeros((parents, LANES), F32)
        imag = jnp.zeros((parents, LANES), F32)
        for octant in range(8):
            s, c = sine[octant : octant + 1], cosine[octant : octant + 1]
            fine_real = fine_ref[pl.ds(octant * 2 * parents, parents), lanes]
            fine_imag = fine_ref[pl.ds((octant * 2 + 1) * parents, parents), lanes]
            real = real + (fine_real * c - fine_imag * s)
            imag = imag + (fine_real * s + fine_imag * c)
        out_ref[0, :, lanes] = real
        out_ref[1, :, lanes] = imag


def count_pairs(lists_ref, kinds, sources, counts_ref):
    slots = lists_ref.shape[3]
    slot = lax.broadcasted_iota(jnp.int32, (1, slots), 1)
    kind = lax.broadcasted_iota(jnp.int32, (kinds, slots), 0)
    source = lax.broadcasted_iota(jnp.int32, (2 * sources, slots), 0) % sources

    @pl.loop(0, counts_ref.shape[0])
    def _(d):
        for p in range(8):
            live = slot < lists_ref[d, 2, pl.ds(p, 1), :]
            kind_hot = ((kind == lists_ref[d, 1, pl.ds(p, 1), :]) & live).astype(F32).astype(BF16)
            source_hot = (source == lists_ref[d, 0, pl.ds(p, 1), :]).astype(F32).astype(BF16)
            pairs = lax.dot_general(
                kind_hot, source_hot, (((1,), (1,)), ((), ())), preferred_element_type=F32
            )
            counts_ref[d, pl.ds(p * kinds, kinds), :] = pairs.astype(BF16)


def load_sources(grid_ref, sources_ref):
    blocks, _, parents, _ = grid_ref.shape
    sources = blocks * parents
    for tile in range(sources_ref.shape[0]):
        lanes = pl.ds(tile * LANES, LANES)
        for b in range(blocks):
            for part in range(2):
                high, low = split(grid_ref[b, part, :, lanes])
                columns = pl.ds(part * LANES, LANES)
                sources_ref[tile, pl.ds(b * parents, parents), columns] = high
                sources_ref[tile, pl.ds(sources + b * parents, parents), columns] = low


def fold(values):
    row = lax.broadcasted_iota(jnp.int32, (8, LANES), 0)
    lower = row < 4
    values = [
        jnp.where(lower, a, b) + pltpu.roll(jnp.where(lower, b, a), 4, axis=0)
        for a, b in zip(values[:4], values[4:])
    ]
    for reach in (2, 1):
        lower = row % (2 * reach) < reach
        values = [
            jnp.where(lower, a + pltpu.roll(a, 8 - reach, axis=0), b + pltpu.roll(b, reach, axis=0))
            for a, b in zip(values[:reach], values[reach:])
        ]
    return values[0]


def multiply_tile(summed_ref, table_ref, column, tile, out_ref):
    kinds = table_ref.shape[1]
    lanes = pl.ds(pl.multiple_of(column + tile * LANES, LANES), LANES)
    groups = range(0, kinds, 8)
    table_real = [table_ref[0, pl.ds(k, 8), lanes] for k in groups]
    table_imag = [table_ref[1, pl.ds(k, 8), lanes] for k in groups]
    reals, imags = [], []
    for p in range(8):
        real, imag = None, None
        for k, tr, ti in zip(groups, table_real, table_imag):
            summed_real = summed_ref[pl.ds(p * kinds + k, 8), pl.ds(0, LANES)]
            summed_imag = summed_ref[pl.ds(p * kinds + k, 8), pl.ds(LANES, LANES)]
            add_real = tr * summed_real - ti * summed_imag
            add_imag = tr * summed_imag + ti * summed_real
            real = add_real if real is None else real + add_real
            imag = add_imag if imag is None else imag + add_imag
        reals.append(real)
        imags.append(imag)
    out_ref[0, :, pl.ds(tile * LANES, LANES)] = fold(reals)
    out_ref[1, :, pl.ds(tile * LANES, LANES)] = fold(imags)


def fused_kernel(
    parents, span, total, ids_in, kinds_in, lengths_in, children_ref, index_in, weight_in, phase_in, table_in, out_ref,
    held_ref, left_ref, right_ref, index_ref, weight_ref, phase_ref, table_ref, lists_ref, spare_ref,
    high_ref, low_ref, high_a, low_a, fine_a, high_b, low_b, fine_b, outgoing_ref, grid_ref,
    counts_ref, sources_ref, summed_even, summed_odd, result_ref, landing_ref,
    load_sems, input_sems, self_sems, halo_send, halo_recv, list_send, list_recv,
    box_send, box_recv, dir_send, dir_recv, place_sems,
):
    tiles = held_ref.shape[0]
    chunks, boxes, _, _, block = grid_ref.shape
    dirs = lists_ref.shape[0]
    kinds = table_ref.shape[1]
    my_box, my_dir = lax.axis_index("box"), lax.axis_index("dir")
    first = my_dir * index_ref.shape[1]
    mesh_type = pl.DeviceIdType.MESH

    def dir_at(step):
        return (my_dir + step + dirs) % dirs

    def box_at(step):
        return (my_box + step + boxes) % boxes

    inputs = [
        pltpu.make_async_copy(source, target, input_sems.at[i])
        for i, (source, target) in enumerate(
            [
                (index_in, index_ref), (weight_in, weight_ref), (phase_in, phase_ref),
                (ids_in, lists_ref.at[my_dir, 0]), (kinds_in, lists_ref.at[my_dir, 1]),
                (lengths_in, spare_ref), (table_in.at[:, :, 0, my_dir], table_ref),
            ]
        )
    ]

    def load(tile):
        return pltpu.make_async_copy(
            children_ref.at[:, :, pl.ds(pl.multiple_of(tile * LANES, LANES), LANES)],
            held_ref.at[tile], load_sems.at[tile],
        )

    @pl.loop(0, tiles)
    def _(tile):
        load(tile).start()

    for copy in inputs:
        copy.start()

    barrier = pltpu.get_barrier_semaphore()

    @pl.loop(1, dirs)
    def _(step):
        pl.semaphore_signal(barrier, inc=1, device_id={"dir": dir_at(step)}, device_id_type=mesh_type)

    @pl.loop(1, boxes)
    def _(step):
        pl.semaphore_signal(barrier, inc=1, device_id={"box": box_at(step)}, device_id_type=mesh_type)

    pl.semaphore_wait(barrier, dirs + boxes - 2)

    halos = [
        pltpu.make_async_remote_copy(
            src_ref=children_ref.at[:, :, pl.ds(column, LANES)], dst_ref=target,
            send_sem=halo_send.at[i], recv_sem=halo_recv.at[i],
            device_id={"dir": dir_at(step)}, device_id_type=mesh_type,
        )
        for i, (column, target, step) in enumerate(
            [((tiles - 1) * LANES, left_ref, 1), (0, right_ref, -1)]
        )
    ]
    for copy in halos:
        copy.start()

    def list_copy(step, owner):
        return pltpu.make_async_remote_copy(
            src_ref=lists_ref.at[my_dir], dst_ref=lists_ref.at[owner],
            send_sem=list_send.at[step], recv_sem=list_recv.at[step],
            device_id={"dir": dir_at(step)}, device_id_type=mesh_type,
        )

    for copy in inputs[3:6]:
        copy.wait()
    square = (8, spare_ref.shape[1])
    own = lax.broadcasted_iota(jnp.int32, square, 0) == lax.broadcasted_iota(jnp.int32, square, 1)
    lengths = jnp.sum(jnp.where(own, spare_ref[...].astype(F32), 0.0), axis=1, keepdims=True)
    lists_ref[my_dir, 2] = jnp.broadcast_to(lengths, (8, lists_ref.shape[3])).astype(jnp.int32)

    @pl.loop(1, dirs)
    def _(step):
        list_copy(step, my_dir).start()

    def box_copy(chunk, step, owner):
        return pltpu.make_async_remote_copy(
            src_ref=outgoing_ref.at[chunk, step], dst_ref=grid_ref.at[chunk, owner],
            send_sem=box_send.at[chunk, step], recv_sem=box_recv.at[chunk, step],
            device_id={"box": box_at(step)}, device_id_type=mesh_type,
        )

    def own_box_copy(chunk):
        return pltpu.make_async_copy(
            outgoing_ref.at[chunk, 0], grid_ref.at[chunk, my_box], self_sems.at[0, chunk]
        )

    def dir_target(chunk, owner):
        return landing_ref.at[owner, :, :, pl.ds(pl.multiple_of(chunk * block, LANES), block)]

    def place(chunk, step):
        lanes = pl.ds(pl.multiple_of(chunk * block, LANES), block)
        return pltpu.make_async_copy(
            dir_target(chunk, dir_at(-step)), out_ref.at[:, :, 0, dir_at(-step), lanes],
            place_sems.at[chunk, step],
        )

    def dir_copy(chunk, step, owner):
        return pltpu.make_async_remote_copy(
            src_ref=result_ref.at[chunk, step], dst_ref=dir_target(chunk, owner),
            send_sem=dir_send.at[chunk, step], recv_sem=dir_recv.at[chunk, step],
            device_id={"dir": dir_at(step)}, device_id_type=mesh_type,
        )

    def own_dir_copy(chunk):
        return pltpu.make_async_copy(
            result_ref.at[chunk, 0], dir_target(chunk, my_dir), self_sems.at[1, chunk]
        )

    def clear():
        for ref in (high_a, low_a, high_b, low_b):
            ref[...] = jnp.zeros_like(ref)

    clear()

    @pl.loop(0, tiles)
    def _(tile):
        load(tile).wait()

    @pl.loop(1, tiles)
    def _(tile):
        prepare_columns(held_ref, left_ref, right_ref, tile, high_ref, low_ref, parents)

    def edges():
        for copy in halos:
            copy.wait_recv()
        prepare_columns(held_ref, left_ref, right_ref, 0, high_ref, low_ref, parents)
        prepare_columns(held_ref, left_ref, right_ref, tiles, high_ref, low_ref, parents)

    def lists():
        @pl.loop(1, dirs)
        def _(step):
            list_copy(step, dir_at(-step)).wait_recv()

        count_pairs(lists_ref, kinds, sources_ref.shape[1] // 2, counts_ref)
        inputs[6].wait()

    for copy in inputs[:3]:
        copy.wait()

    def aggregate(chunk):
        @pl.loop(0, boxes // 2)
        def _(pair):
            steps = (2 * pair + 1, (2 * pair + 2) % boxes)
            if block != 512:
                clear()
            work = []
            for step, buffers in zip(steps, ((high_a, low_a, fine_a), (high_b, low_b, fine_b))):
                start = pl.multiple_of(box_at(step) * span + chunk * block, LANES)
                coarse = start // 4
                if block == 512:
                    base, shift = pl.multiple_of(coarse, LANES), 0
                else:
                    base = pl.multiple_of(coarse // LANES * LANES, LANES)
                    shift = coarse % LANES
                work.append((start, base, shift, step) + buffers)
            for start, base, shift, step, band_high, band_low, fine_ref in work:
                band_matrix(index_ref, weight_ref, start, first, shift, block, total, band_high, band_low)
            for start, base, shift, step, band_high, band_low, fine_ref in work:
                interpolate(high_ref, low_ref, base, band_high, band_low, fine_ref)
            for start, base, shift, step, band_high, band_low, fine_ref in work:
                rotate(phase_ref, start, fine_ref, parents, outgoing_ref.at[chunk, step])
            box_copy(chunk, steps[0], my_box).start()

            @pl.when(steps[1] > 0)
            def _():
                box_copy(chunk, steps[1], my_box).start()

        own_box_copy(chunk).start()

    def translate(chunk):
        own_box_copy(chunk).wait()

        @pl.loop(1, boxes)
        def _(step):
            box_copy(chunk, step, box_at(-step)).wait_recv()

        load_sources(grid_ref.at[chunk], sources_ref)
        count = sources_ref.shape[0]
        buffers = (summed_even, summed_odd)

        def sum_tile(d, tile, buffer):
            buffer[...] = jnp.dot(counts_ref[d], sources_ref[tile], preferred_element_type=F32)

        def items(step, parity):
            for tile in range(count):
                if tile + 1 < count:
                    sum_tile(dir_at(step), tile + 1, buffers[(parity + tile + 1) % 2])
                else:
                    sum_tile(dir_at(step + 1), 0, buffers[(parity + tile + 1) % 2])
                multiply_tile(
                    buffers[(parity + tile) % 2], table_ref, chunk * block, tile, result_ref.at[chunk, step]
                )

        def send(step):
            @pl.when(step > 0)
            def _():
                dir_copy(chunk, step, my_dir).start()

        sum_tile(dir_at(1), 0, summed_even)
        if count % 2 == 0:

            @pl.loop(0, dirs)
            def _(turn):
                step = (turn + 1) % dirs
                items(step, 0)
                send(step)

        else:

            @pl.loop(0, dirs // 2)
            def _(turn):
                for half in range(2):
                    step = (2 * turn + half + 1) % dirs
                    items(step, half)
                    send(step)

        own_dir_copy(chunk).start()

    if chunks < 3:
        edges()

    @pl.loop(0, chunks + 1)
    def _(turn):
        if chunks >= 3:
            pl.when(turn == chunks - 2)(edges)

        @pl.when(turn < chunks)
        def _():
            aggregate((turn + 1) % chunks)

        @pl.when(turn == 0)
        def _():
            lists()

        @pl.when(turn > 0)
        def _():
            translate(turn % chunks)

    for copy in halos:
        copy.wait_send()

    @pl.loop(1, dirs)
    def _(step):
        list_copy(step, my_dir).wait_send()

    @pl.loop(0, chunks)
    def _(turn):
        chunk = (turn + 1) % chunks
        own_dir_copy(chunk).wait()
        place(chunk, 0).start()

        @pl.loop(1, dirs)
        def _(step):
            dir_copy(chunk, step, dir_at(-step)).wait_recv()
            place(chunk, step).start()

        @pl.loop(1, boxes)
        def _(step):
            box_copy(chunk, step, my_box).wait_send()

    @pl.loop(0, chunks)
    def _(chunk):
        @pl.loop(1, dirs)
        def _(step):
            dir_copy(chunk, step, my_dir).wait_send()

        @pl.loop(0, dirs)
        def _(step):
            place(chunk, step).wait()


def on_device(
    children, stencil_index, stencil_weights, child_phase, translations, box_lengths, partner_ids, partner_kinds
):
    boxes = lax.axis_size("box")
    dirs = lax.axis_size("dir")
    rows, coarse = children.shape[1:]
    fine = stencil_index.shape[1]
    parents = rows // 8
    span = fine // boxes
    kinds = translations.shape[1]
    sources = parents * boxes
    slots = partner_ids.shape[1]
    block, depth = block_layout(fine, span)
    chunks = span // block
    vmem, dma = pltpu.VMEM, pltpu.SemaphoreType.DMA
    return pl.pallas_call(
        functools.partial(fused_kernel, parents, span, coarse * dirs),
        out_shape=jax.ShapeDtypeStruct((2, 8, 1, dirs, span), F32),
        in_specs=[pl.BlockSpec(memory_space=pl.ANY)] * 8,
        out_specs=pl.BlockSpec(memory_space=pl.ANY),
        scratch_shapes=[
            vmem((coarse // LANES, 2, rows, LANES), F32),
            vmem((2, rows, LANES), F32),
            vmem((2, rows, LANES), F32),
            vmem(stencil_index.shape, jnp.int32),
            vmem(stencil_weights.shape, F32),
            vmem(child_phase.shape, F32),
            vmem((2, kinds, span), F32),
            vmem((dirs, 3, 8, slots), jnp.int32),
            vmem((1, box_lengths.shape[0]), jnp.int32),
            vmem((2 * rows, coarse + LANES), BF16),
            vmem((2 * rows, coarse + LANES), BF16),
            vmem((depth, block), BF16),
            vmem((depth, block), BF16),
            vmem((2 * rows, block), F32),
            vmem((depth, block), BF16),
            vmem((depth, block), BF16),
            vmem((2 * rows, block), F32),
            vmem((chunks, boxes, 2, parents, block), F32),
            vmem((chunks, boxes, 2, parents, block), F32),
            vmem((dirs, kinds * 8, 2 * sources), BF16),
            vmem((block // LANES, 2 * sources, 2 * LANES), BF16),
            vmem((kinds * 8, 2 * LANES), F32),
            vmem((kinds * 8, 2 * LANES), F32),
            vmem((chunks, dirs, 2, 8, block), F32),
            vmem((dirs, 2, 8, span), F32),
            dma((coarse // LANES,)),
            dma((7,)),
            dma((2, chunks)),
            dma((2,)),
            dma((2,)),
            dma((dirs,)),
            dma((dirs,)),
            dma((chunks, boxes)),
            dma((chunks, boxes)),
            dma((chunks, dirs)),
            dma((chunks, dirs)),
            dma((chunks, dirs)),
        ],
        compiler_params=pltpu.CompilerParams(
            collective_id=0, has_side_effects=True, vmem_limit_bytes=56 << 20
        ),
    )(partner_ids, partner_kinds, box_lengths.reshape(1, -1), children, stencil_index, stencil_weights, child_phase, translations)


def solution(mesh):
    return jax.shard_map(
        on_device,
        mesh=mesh,
        in_specs=(
            P(None, "box", "dir"),
            P(None, "dir"),
            P(None, "dir"),
            P(None, "dir"),
            P(None, None, "box", None, None),
            P("dir"),
            P("dir", None),
            P("dir", None),
        ),
        out_specs=P(None, "dir", "box", None, None),
        check_vma=False,
    )
```

```python
import functools

import jax
import jax.numpy as jnp
from jax import lax
from jax.experimental import pallas as pl
from jax.experimental.pallas import tpu as pltpu
from jax.sharding import PartitionSpec as P

LANES = 128
F32 = jnp.float32
BF16 = jnp.bfloat16
SIN_TERMS = (1.0, -1 / 6, 1 / 120, -1 / 5040, 1 / 362880, -1 / 39916800, 1 / 6227020800)
COS_TERMS = (1.0, -1 / 2, 1 / 24, -1 / 720, 1 / 40320, -1 / 3628800, 1 / 479001600)


def split(value):
    high = value.astype(BF16)
    return high, (value - high.astype(F32)).astype(BF16)


def series(terms, square):
    total = jnp.full_like(square, terms[-1])
    for term in terms[-2::-1]:
        total = total * square + term
    return total


def sine_cosine(angle):
    half = angle * 0.5
    square = half * half
    sine = half * series(SIN_TERMS, square)
    cosine = series(COS_TERMS, square)
    return 2.0 * sine * cosine, 1.0 - 2.0 * sine * sine


def shifted_tile(before, tile):
    lane = lax.broadcasted_iota(jnp.int32, tile.shape, 1)
    return jnp.where(lane < 2, pltpu.roll(before, 2, axis=1), pltpu.roll(tile, 2, axis=1))


def rows_of(ref, part, octant, parents):
    return ref[part, pl.ds(octant, parents, stride=8), :]


def prepare_columns(held_ref, left_ref, right_ref, tile, high_ref, low_ref, parents):
    tiles = held_ref.shape[0]
    edge = isinstance(tile, int)
    here = right_ref if edge and tile == tiles else held_ref.at[tile]
    before = left_ref if edge and tile == 0 else held_ref.at[tile - 1]
    column = tile * LANES if edge else pl.multiple_of(tile * LANES, LANES)
    for octant in range(8):
        for part in range(2):
            moved = shifted_tile(
                rows_of(before, part, octant, parents), rows_of(here, part, octant, parents)
            )
            high, low = split(moved)
            rows = pl.ds((octant * 2 + part) * parents, parents)
            high_ref[rows, pl.ds(column, LANES)] = high
            low_ref[rows, pl.ds(column, LANES)] = low


def block_layout(width, span):
    block = 512 if span % 512 == 0 else span
    return block, (256 if block == 512 else -(-(block // 4 + 128) // LANES) * LANES)


def band_matrix(index_ref, weight_ref, start, first, shift, block, total, high_ref, low_ref):
    lane = lax.broadcasted_iota(jnp.int32, (1, LANES), 1) // 4
    row = lax.broadcasted_iota(jnp.int32, (48, LANES), 0)
    for tile in range(block // LANES):
        column = pl.multiple_of(start + tile * LANES, LANES)
        centre = (first + start + tile * LANES) // 4 + lane
        band = jnp.zeros((48, LANES), F32)
        for point in range(index_ref.shape[0]):
            offset = index_ref[pl.ds(point, 1), pl.ds(column, LANES)] - centre + 2
            offset = jnp.where(offset < 0, offset + total, offset)
            offset = jnp.where(offset >= total, offset - total, offset) + lane
            band = band + jnp.where(row == offset, weight_ref[pl.ds(point, 1), pl.ds(column, LANES)], 0.0)
        high, low = split(band)
        rows = pl.ds(pl.multiple_of(shift + tile * 32, 32), 48)
        high_ref[rows, pl.ds(tile * LANES, LANES)] = high
        low_ref[rows, pl.ds(tile * LANES, LANES)] = low


def interpolate(high_ref, low_ref, base, band_high, band_low, fine_ref):
    window = pl.ds(base, band_high.shape[0])
    lhs = jnp.concatenate([high_ref[:, window], high_ref[:, window], low_ref[:, window]], axis=1)
    rhs = jnp.concatenate([band_high[...], band_low[...], band_high[...]], axis=0)
    fine_ref[...] = jnp.dot(lhs, rhs, preferred_element_type=F32)


def rotate(phase_ref, start, fine_ref, parents, out_ref):
    for tile in range(fine_ref.shape[1] // LANES):
        lanes = pl.ds(tile * LANES, LANES)
        sine, cosine = sine_cosine(phase_ref[:, pl.ds(pl.multiple_of(start + tile * LANES, LANES), LANES)])
        real = jnp.zeros((parents, LANES), F32)
        imag = jnp.zeros((parents, LANES), F32)
        for octant in range(8):
            s, c = sine[octant : octant + 1], cosine[octant : octant + 1]
            fine_real = fine_ref[pl.ds(octant * 2 * parents, parents), lanes]
            fine_imag = fine_ref[pl.ds((octant * 2 + 1) * parents, parents), lanes]
            real = real + (fine_real * c - fine_imag * s)
            imag = imag + (fine_real * s + fine_imag * c)
        out_ref[0, :, lanes] = real
        out_ref[1, :, lanes] = imag


def count_pairs(lists_ref, kinds, sources, counts_ref):
    slots = lists_ref.shape[3]
    slot = lax.broadcasted_iota(jnp.int32, (1, slots), 1)
    kind = lax.broadcasted_iota(jnp.int32, (kinds, slots), 0)
    source = lax.broadcasted_iota(jnp.int32, (2 * sources, slots), 0) % sources

    @pl.loop(0, counts_ref.shape[0])
    def _(d):
        for p in range(8):
            live = slot < lists_ref[d, 2, pl.ds(p, 1), :]
            kind_hot = ((kind == lists_ref[d, 1, pl.ds(p, 1), :]) & live).astype(F32).astype(BF16)
            source_hot = (source == lists_ref[d, 0, pl.ds(p, 1), :]).astype(F32).astype(BF16)
            pairs = lax.dot_general(
                kind_hot, source_hot, (((1,), (1,)), ((), ())), preferred_element_type=F32
            )
            counts_ref[d, pl.ds(p * kinds, kinds), :] = pairs.astype(BF16)


def load_sources(grid_ref, sources_ref):
    blocks, _, parents, _ = grid_ref.shape
    sources = blocks * parents
    for tile in range(sources_ref.shape[0]):
        lanes = pl.ds(tile * LANES, LANES)
        for b in range(blocks):
            for part in range(2):
                high, low = split(grid_ref[b, part, :, lanes])
                columns = pl.ds(part * LANES, LANES)
                sources_ref[tile, pl.ds(b * parents, parents), columns] = high
                sources_ref[tile, pl.ds(sources + b * parents, parents), columns] = low


def fold(values):
    row = lax.broadcasted_iota(jnp.int32, (8, LANES), 0)
    lower = row < 4
    values = [
        jnp.where(lower, a, b) + pltpu.roll(jnp.where(lower, b, a), 4, axis=0)
        for a, b in zip(values[:4], values[4:])
    ]
    for reach in (2, 1):
        lower = row % (2 * reach) < reach
        values = [
            jnp.where(lower, a + pltpu.roll(a, 8 - reach, axis=0), b + pltpu.roll(b, reach, axis=0))
            for a, b in zip(values[:reach], values[reach:])
        ]
    return values[0]


def multiply_tile(summed_ref, table_ref, column, tile, out_ref):
    kinds = table_ref.shape[1]
    lanes = pl.ds(pl.multiple_of(column + tile * LANES, LANES), LANES)
    groups = range(0, kinds, 8)
    table_real = [table_ref[0, pl.ds(k, 8), lanes] for k in groups]
    table_imag = [table_ref[1, pl.ds(k, 8), lanes] for k in groups]
    reals, imags = [], []
    for p in range(8):
        real, imag = None, None
        for k, tr, ti in zip(groups, table_real, table_imag):
            summed_real = summed_ref[pl.ds(p * kinds + k, 8), pl.ds(0, LANES)]
            summed_imag = summed_ref[pl.ds(p * kinds + k, 8), pl.ds(LANES, LANES)]
            add_real = tr * summed_real - ti * summed_imag
            add_imag = tr * summed_imag + ti * summed_real
            real = add_real if real is None else real + add_real
            imag = add_imag if imag is None else imag + add_imag
        reals.append(real)
        imags.append(imag)
    out_ref[0, :, pl.ds(tile * LANES, LANES)] = fold(reals)
    out_ref[1, :, pl.ds(tile * LANES, LANES)] = fold(imags)


def fused_kernel(
    parents, span, total, ids_in, kinds_in, lengths_in, children_ref, index_in, weight_in, phase_in, table_in, out_ref,
    held_ref, left_ref, right_ref, index_ref, weight_ref, phase_ref, table_ref, lists_ref, spare_ref,
    high_ref, low_ref, high_a, low_a, fine_a, high_b, low_b, fine_b, outgoing_ref, grid_ref,
    counts_ref, sources_ref, summed_even, summed_odd, result_ref, landing_ref,
    load_sems, input_sems, self_sems, halo_send, halo_recv, list_send, list_recv,
    box_send, box_recv, dir_send, dir_recv, place_sems,
):
    tiles = held_ref.shape[0]
    chunks, boxes, _, _, block = grid_ref.shape
    dirs = lists_ref.shape[0]
    kinds = table_ref.shape[1]
    my_box, my_dir = lax.axis_index("box"), lax.axis_index("dir")
    first = my_dir * index_ref.shape[1]
    mesh_type = pl.DeviceIdType.MESH

    def dir_at(step):
        return (my_dir + step + dirs) % dirs

    def box_at(step):
        return (my_box + step + boxes) % boxes

    inputs = [
        pltpu.make_async_copy(source, target, input_sems.at[i])
        for i, (source, target) in enumerate(
            [
                (index_in, index_ref), (weight_in, weight_ref), (phase_in, phase_ref),
                (ids_in, lists_ref.at[my_dir, 0]), (kinds_in, lists_ref.at[my_dir, 1]),
                (lengths_in, spare_ref), (table_in.at[:, :, 0, my_dir], table_ref),
            ]
        )
    ]

    def load(tile):
        return pltpu.make_async_copy(
            children_ref.at[:, :, pl.ds(pl.multiple_of(tile * LANES, LANES), LANES)],
            held_ref.at[tile], load_sems.at[tile],
        )

    per = tiles // boxes
    early = (0, 1, 2) if chunks >= 3 else tuple(range(per))
    late = tuple(range(3, per)) if chunks >= 3 else ()

    def over_sections(offsets, act):
        @pl.loop(0, boxes)
        def _(section):
            for offset in offsets:
                act(section * per + offset)

    def prepare(tile):
        prepare_columns(held_ref, left_ref, right_ref, tile, high_ref, low_ref, parents)

    over_sections(early, lambda tile: load(tile).start())
    for copy in inputs[3:6] + inputs[:3]:
        copy.start()
    over_sections(late, lambda tile: load(tile).start())
    inputs[6].start()

    barrier = pltpu.get_barrier_semaphore()

    @pl.loop(1, dirs)
    def _(step):
        pl.semaphore_signal(barrier, inc=1, device_id={"dir": dir_at(step)}, device_id_type=mesh_type)

    @pl.loop(1, boxes)
    def _(step):
        pl.semaphore_signal(barrier, inc=1, device_id={"box": box_at(step)}, device_id_type=mesh_type)

    def clear():
        for ref in (high_a, low_a, high_b, low_b):
            ref[...] = jnp.zeros_like(ref)

    clear()
    over_sections(early, lambda tile: load(tile).wait())
    if chunks >= 3:
        over_sections((1, 2), prepare)
    else:

        @pl.loop(1, tiles)
        def _(tile):
            prepare(tile)

    pl.semaphore_wait(barrier, dirs + boxes - 2)

    halos = [
        pltpu.make_async_remote_copy(
            src_ref=children_ref.at[:, :, pl.ds(column, LANES)], dst_ref=target,
            send_sem=halo_send.at[i], recv_sem=halo_recv.at[i],
            device_id={"dir": dir_at(step)}, device_id_type=mesh_type,
        )
        for i, (column, target, step) in enumerate(
            [((tiles - 1) * LANES, left_ref, 1), (0, right_ref, -1)]
        )
    ]
    for copy in halos:
        copy.start()

    def list_copy(step, owner):
        return pltpu.make_async_remote_copy(
            src_ref=lists_ref.at[my_dir], dst_ref=lists_ref.at[owner],
            send_sem=list_send.at[step], recv_sem=list_recv.at[step],
            device_id={"dir": dir_at(step)}, device_id_type=mesh_type,
        )

    for copy in inputs[3:6]:
        copy.wait()
    square = (8, spare_ref.shape[1])
    own = lax.broadcasted_iota(jnp.int32, square, 0) == lax.broadcasted_iota(jnp.int32, square, 1)
    lengths = jnp.sum(jnp.where(own, spare_ref[...].astype(F32), 0.0), axis=1, keepdims=True)
    lists_ref[my_dir, 2] = jnp.broadcast_to(lengths, (8, lists_ref.shape[3])).astype(jnp.int32)

    @pl.loop(1, dirs)
    def _(step):
        list_copy(step, my_dir).start()

    def box_copy(chunk, step, owner):
        return pltpu.make_async_remote_copy(
            src_ref=outgoing_ref.at[chunk, step], dst_ref=grid_ref.at[chunk, owner],
            send_sem=box_send.at[chunk, step], recv_sem=box_recv.at[chunk, step],
            device_id={"box": box_at(step)}, device_id_type=mesh_type,
        )

    def own_box_copy(chunk):
        return pltpu.make_async_copy(
            outgoing_ref.at[chunk, 0], grid_ref.at[chunk, my_box], self_sems.at[0, chunk]
        )

    def dir_target(chunk, owner):
        return landing_ref.at[owner, :, :, pl.ds(pl.multiple_of(chunk * block, LANES), block)]

    def place(chunk, step):
        lanes = pl.ds(pl.multiple_of(chunk * block, LANES), block)
        return pltpu.make_async_copy(
            dir_target(chunk, dir_at(-step)), out_ref.at[:, :, 0, dir_at(-step), lanes],
            place_sems.at[chunk, step],
        )

    def dir_copy(chunk, step, owner):
        return pltpu.make_async_remote_copy(
            src_ref=result_ref.at[chunk, step], dst_ref=dir_target(chunk, owner),
            send_sem=dir_send.at[chunk, step], recv_sem=dir_recv.at[chunk, step],
            device_id={"dir": dir_at(step)}, device_id_type=mesh_type,
        )

    def own_dir_copy(chunk):
        return pltpu.make_async_copy(
            result_ref.at[chunk, 0], dir_target(chunk, my_dir), self_sems.at[1, chunk]
        )

    def rest():
        over_sections(late, lambda tile: load(tile).wait())
        over_sections(late, prepare)

        @pl.loop(1, boxes)
        def _(section):
            prepare(section * per)

    def edges():
        for copy in halos:
            copy.wait_recv()
        prepare_columns(held_ref, left_ref, right_ref, 0, high_ref, low_ref, parents)
        prepare_columns(held_ref, left_ref, right_ref, tiles, high_ref, low_ref, parents)

    def lists():
        @pl.loop(1, dirs)
        def _(step):
            list_copy(step, dir_at(-step)).wait_recv()

        count_pairs(lists_ref, kinds, sources_ref.shape[1] // 2, counts_ref)
        inputs[6].wait()

    for copy in inputs[:3]:
        copy.wait()

    def aggregate(chunk):
        @pl.loop(0, boxes // 2)
        def _(pair):
            steps = (2 * pair + 1, (2 * pair + 2) % boxes)
            if block != 512:
                clear()
            work = []
            for step, buffers in zip(steps, ((high_a, low_a, fine_a), (high_b, low_b, fine_b))):
                start = pl.multiple_of(box_at(step) * span + chunk * block, LANES)
                coarse = start // 4
                if block == 512:
                    base, shift = pl.multiple_of(coarse, LANES), 0
                else:
                    base = pl.multiple_of(coarse // LANES * LANES, LANES)
                    shift = coarse % LANES
                work.append((start, base, shift, step) + buffers)
            for start, base, shift, step, band_high, band_low, fine_ref in work:
                band_matrix(index_ref, weight_ref, start, first, shift, block, total, band_high, band_low)
            for start, base, shift, step, band_high, band_low, fine_ref in work:
                interpolate(high_ref, low_ref, base, band_high, band_low, fine_ref)
            for start, base, shift, step, band_high, band_low, fine_ref in work:
                rotate(phase_ref, start, fine_ref, parents, outgoing_ref.at[chunk, step])
            box_copy(chunk, steps[0], my_box).start()

            @pl.when(steps[1] > 0)
            def _():
                box_copy(chunk, steps[1], my_box).start()

        own_box_copy(chunk).start()

    def translate(chunk):
        own_box_copy(chunk).wait()

        @pl.loop(1, boxes)
        def _(step):
            box_copy(chunk, step, box_at(-step)).wait_recv()

        load_sources(grid_ref.at[chunk], sources_ref)
        count = sources_ref.shape[0]
        buffers = (summed_even, summed_odd)

        def sum_tile(d, tile, buffer):
            buffer[...] = jnp.dot(counts_ref[d], sources_ref[tile], preferred_element_type=F32)

        def items(step, parity):
            for tile in range(count):
                if tile + 1 < count:
                    sum_tile(dir_at(step), tile + 1, buffers[(parity + tile + 1) % 2])
                else:
                    sum_tile(dir_at(step + 1), 0, buffers[(parity + tile + 1) % 2])
                multiply_tile(
                    buffers[(parity + tile) % 2], table_ref, chunk * block, tile, result_ref.at[chunk, step]
                )

        def send(step):
            @pl.when(step > 0)
            def _():
                dir_copy(chunk, step, my_dir).start()

        sum_tile(dir_at(1), 0, summed_even)
        if count % 2 == 0:

            @pl.loop(0, dirs)
            def _(turn):
                step = (turn + 1) % dirs
                items(step, 0)
                send(step)

        else:

            @pl.loop(0, dirs // 2)
            def _(turn):
                for half in range(2):
                    step = (2 * turn + half + 1) % dirs
                    items(step, half)
                    send(step)

        own_dir_copy(chunk).start()

    if chunks < 3:
        edges()

    @pl.loop(0, chunks + 1)
    def _(turn):
        if chunks >= 3:
            pl.when(turn == chunks - 2)(edges)

        @pl.when(turn < chunks)
        def _():
            aggregate((turn + 1) % chunks)

        @pl.when(turn == 0)
        def _():
            if chunks >= 3:
                rest()
            lists()

        @pl.when(turn > 0)
        def _():
            translate(turn % chunks)

    for copy in halos:
        copy.wait_send()

    @pl.loop(1, dirs)
    def _(step):
        list_copy(step, my_dir).wait_send()

    @pl.loop(0, chunks)
    def _(turn):
        chunk = (turn + 1) % chunks
        own_dir_copy(chunk).wait()
        place(chunk, 0).start()

        @pl.loop(1, dirs)
        def _(step):
            dir_copy(chunk, step, dir_at(-step)).wait_recv()
            place(chunk, step).start()

        @pl.loop(1, boxes)
        def _(step):
            box_copy(chunk, step, my_box).wait_send()

    @pl.loop(0, chunks)
    def _(chunk):
        @pl.loop(1, dirs)
        def _(step):
            dir_copy(chunk, step, my_dir).wait_send()

        @pl.loop(0, dirs)
        def _(step):
            place(chunk, step).wait()


def on_device(
    children, stencil_index, stencil_weights, child_phase, translations, box_lengths, partner_ids, partner_kinds
):
    boxes = lax.axis_size("box")
    dirs = lax.axis_size("dir")
    rows, coarse = children.shape[1:]
    fine = stencil_index.shape[1]
    parents = rows // 8
    span = fine // boxes
    kinds = translations.shape[1]
    sources = parents * boxes
    slots = partner_ids.shape[1]
    block, depth = block_layout(fine, span)
    chunks = span // block
    vmem, dma = pltpu.VMEM, pltpu.SemaphoreType.DMA
    return pl.pallas_call(
        functools.partial(fused_kernel, parents, span, coarse * dirs),
        out_shape=jax.ShapeDtypeStruct((2, 8, 1, dirs, span), F32),
        in_specs=[pl.BlockSpec(memory_space=pl.ANY)] * 8,
        out_specs=pl.BlockSpec(memory_space=pl.ANY),
        scratch_shapes=[
            vmem((coarse // LANES, 2, rows, LANES), F32),
            vmem((2, rows, LANES), F32),
            vmem((2, rows, LANES), F32),
            vmem(stencil_index.shape, jnp.int32),
            vmem(stencil_weights.shape, F32),
            vmem(child_phase.shape, F32),
            vmem((2, kinds, span), F32),
            vmem((dirs, 3, 8, slots), jnp.int32),
            vmem((1, box_lengths.shape[0]), jnp.int32),
            vmem((2 * rows, coarse + LANES), BF16),
            vmem((2 * rows, coarse + LANES), BF16),
            vmem((depth, block), BF16),
            vmem((depth, block), BF16),
            vmem((2 * rows, block), F32),
            vmem((depth, block), BF16),
            vmem((depth, block), BF16),
            vmem((2 * rows, block), F32),
            vmem((chunks, boxes, 2, parents, block), F32),
            vmem((chunks, boxes, 2, parents, block), F32),
            vmem((dirs, kinds * 8, 2 * sources), BF16),
            vmem((block // LANES, 2 * sources, 2 * LANES), BF16),
            vmem((kinds * 8, 2 * LANES), F32),
            vmem((kinds * 8, 2 * LANES), F32),
            vmem((chunks, dirs, 2, 8, block), F32),
            vmem((dirs, 2, 8, span), F32),
            dma((coarse // LANES,)),
            dma((7,)),
            dma((2, chunks)),
            dma((2,)),
            dma((2,)),
            dma((dirs,)),
            dma((dirs,)),
            dma((chunks, boxes)),
            dma((chunks, boxes)),
            dma((chunks, dirs)),
            dma((chunks, dirs)),
            dma((chunks, dirs)),
        ],
        compiler_params=pltpu.CompilerParams(
            collective_id=0, has_side_effects=True, vmem_limit_bytes=56 << 20
        ),
    )(partner_ids, partner_kinds, box_lengths.reshape(1, -1), children, stencil_index, stencil_weights, child_phase, translations)


def solution(mesh):
    return jax.shard_map(
        on_device,
        mesh=mesh,
        in_specs=(
            P(None, "box", "dir"),
            P(None, "dir"),
            P(None, "dir"),
            P(None, "dir"),
            P(None, None, "box", None, None),
            P("dir"),
            P("dir", None),
            P("dir", None),
        ),
        out_specs=P(None, "dir", "box", None, None),
        check_vma=False,
    )
```

```python
import functools

import jax
import jax.numpy as jnp
from jax import lax
from jax.experimental import pallas as pl
from jax.experimental.pallas import tpu as pltpu
from jax.sharding import PartitionSpec as P

LANES = 128
F32 = jnp.float32
BF16 = jnp.bfloat16
SIN_TERMS = (1.0, -1 / 6, 1 / 120, -1 / 5040, 1 / 362880, -1 / 39916800, 1 / 6227020800)
COS_TERMS = (1.0, -1 / 2, 1 / 24, -1 / 720, 1 / 40320, -1 / 3628800, 1 / 479001600)


def split(value):
    high = value.astype(BF16)
    return high, (value - high.astype(F32)).astype(BF16)


def series(terms, square):
    total = jnp.full_like(square, terms[-1])
    for term in terms[-2::-1]:
        total = total * square + term
    return total


def sine_cosine(angle):
    half = angle * 0.5
    square = half * half
    sine = half * series(SIN_TERMS, square)
    cosine = series(COS_TERMS, square)
    return 2.0 * sine * cosine, 1.0 - 2.0 * sine * sine


def shifted_tile(before, tile):
    lane = lax.broadcasted_iota(jnp.int32, tile.shape, 1)
    return jnp.where(lane < 2, pltpu.roll(before, 2, axis=1), pltpu.roll(tile, 2, axis=1))


def rows_of(ref, part, octant, parents):
    return ref[part, pl.ds(octant, parents, stride=8), :]


def prepare_columns(held_ref, left_ref, right_ref, tile, high_ref, low_ref, parents):
    tiles = held_ref.shape[0]
    edge = isinstance(tile, int)
    here = right_ref if edge and tile == tiles else held_ref.at[tile]
    before = left_ref if edge and tile == 0 else held_ref.at[tile - 1]
    column = tile * LANES if edge else pl.multiple_of(tile * LANES, LANES)
    for octant in range(8):
        for part in range(2):
            moved = shifted_tile(
                rows_of(before, part, octant, parents), rows_of(here, part, octant, parents)
            )
            high, low = split(moved)
            rows = pl.ds((octant * 2 + part) * parents, parents)
            high_ref[rows, pl.ds(column, LANES)] = high
            low_ref[rows, pl.ds(column, LANES)] = low


def block_layout(width, span):
    block = 512 if span % 512 == 0 else span
    return block, (256 if block == 512 else -(-(block // 4 + 128) // LANES) * LANES)


def band_matrix(index_ref, weight_ref, start, first, shift, block, total, high_ref, low_ref):
    lane = lax.broadcasted_iota(jnp.int32, (1, LANES), 1) // 4
    row = lax.broadcasted_iota(jnp.int32, (48, LANES), 0)
    for tile in range(block // LANES):
        column = pl.multiple_of(start + tile * LANES, LANES)
        centre = (first + start + tile * LANES) // 4 + lane
        band = jnp.zeros((48, LANES), F32)
        for point in range(index_ref.shape[0]):
            offset = index_ref[pl.ds(point, 1), pl.ds(column, LANES)] - centre + 2
            offset = jnp.where(offset < 0, offset + total, offset)
            offset = jnp.where(offset >= total, offset - total, offset) + lane
            band = band + jnp.where(row == offset, weight_ref[pl.ds(point, 1), pl.ds(column, LANES)], 0.0)
        high, low = split(band)
        rows = pl.ds(pl.multiple_of(shift + tile * 32, 32), 48)
        high_ref[rows, pl.ds(tile * LANES, LANES)] = high
        low_ref[rows, pl.ds(tile * LANES, LANES)] = low


def interpolate(high_ref, low_ref, base, band_high, band_low, fine_ref):
    window = pl.ds(base, band_high.shape[0])
    lhs = jnp.concatenate([high_ref[:, window], high_ref[:, window], low_ref[:, window]], axis=1)
    rhs = jnp.concatenate([band_high[...], band_low[...], band_high[...]], axis=0)
    fine_ref[...] = jnp.dot(lhs, rhs, preferred_element_type=F32)


def rotate(phase_ref, start, fine_ref, parents, out_ref):
    for tile in range(fine_ref.shape[1] // LANES):
        lanes = pl.ds(tile * LANES, LANES)
        sine, cosine = sine_cosine(phase_ref[:, pl.ds(pl.multiple_of(start + tile * LANES, LANES), LANES)])
        real = jnp.zeros((parents, LANES), F32)
        imag = jnp.zeros((parents, LANES), F32)
        for octant in range(8):
            s, c = sine[octant : octant + 1], cosine[octant : octant + 1]
            fine_real = fine_ref[pl.ds(octant * 2 * parents, parents), lanes]
            fine_imag = fine_ref[pl.ds((octant * 2 + 1) * parents, parents), lanes]
            real = real + (fine_real * c - fine_imag * s)
            imag = imag + (fine_real * s + fine_imag * c)
        out_ref[0, :, lanes] = real
        out_ref[1, :, lanes] = imag


def count_pairs(lists_ref, kinds, sources, counts_ref):
    slots = lists_ref.shape[3]
    slot = lax.broadcasted_iota(jnp.int32, (1, slots), 1)
    kind = lax.broadcasted_iota(jnp.int32, (kinds, slots), 0)
    source = lax.broadcasted_iota(jnp.int32, (2 * sources, slots), 0) % sources

    @pl.loop(0, counts_ref.shape[0])
    def _(d):
        for p in range(8):
            live = slot < lists_ref[d, 2, pl.ds(p, 1), :]
            kind_hot = ((kind == lists_ref[d, 1, pl.ds(p, 1), :]) & live).astype(F32).astype(BF16)
            source_hot = (source == lists_ref[d, 0, pl.ds(p, 1), :]).astype(F32).astype(BF16)
            pairs = lax.dot_general(
                kind_hot, source_hot, (((1,), (1,)), ((), ())), preferred_element_type=F32
            )
            counts_ref[d, pl.ds(p * kinds, kinds), :] = pairs.astype(BF16)


def load_sources(grid_ref, sources_ref):
    blocks, _, parents, _ = grid_ref.shape
    sources = blocks * parents
    for tile in range(sources_ref.shape[0]):
        lanes = pl.ds(tile * LANES, LANES)
        for b in range(blocks):
            for part in range(2):
                high, low = split(grid_ref[b, part, :, lanes])
                columns = pl.ds(part * LANES, LANES)
                sources_ref[tile, pl.ds(b * parents, parents), columns] = high
                sources_ref[tile, pl.ds(sources + b * parents, parents), columns] = low


def fold(values):
    row = lax.broadcasted_iota(jnp.int32, (8, LANES), 0)
    lower = row < 4
    values = [
        jnp.where(lower, a, b) + pltpu.roll(jnp.where(lower, b, a), 4, axis=0)
        for a, b in zip(values[:4], values[4:])
    ]
    for reach in (2, 1):
        lower = row % (2 * reach) < reach
        values = [
            jnp.where(lower, a + pltpu.roll(a, 8 - reach, axis=0), b + pltpu.roll(b, reach, axis=0))
            for a, b in zip(values[:reach], values[reach:])
        ]
    return values[0]


def multiply_tile(summed_ref, table_ref, column, tile, out_ref):
    kinds = table_ref.shape[1]
    lanes = pl.ds(pl.multiple_of(column + tile * LANES, LANES), LANES)
    groups = range(0, kinds, 8)
    table_real = [table_ref[0, pl.ds(k, 8), lanes] for k in groups]
    table_imag = [table_ref[1, pl.ds(k, 8), lanes] for k in groups]
    reals, imags = [], []
    for p in range(8):
        real, imag = None, None
        for k, tr, ti in zip(groups, table_real, table_imag):
            summed_real = summed_ref[pl.ds(p * kinds + k, 8), pl.ds(0, LANES)]
            summed_imag = summed_ref[pl.ds(p * kinds + k, 8), pl.ds(LANES, LANES)]
            add_real = tr * summed_real - ti * summed_imag
            add_imag = tr * summed_imag + ti * summed_real
            real = add_real if real is None else real + add_real
            imag = add_imag if imag is None else imag + add_imag
        reals.append(real)
        imags.append(imag)
    out_ref[0, :, pl.ds(tile * LANES, LANES)] = fold(reals)
    out_ref[1, :, pl.ds(tile * LANES, LANES)] = fold(imags)


def fused_kernel(
    parents, span, total, ids_in, kinds_in, lengths_in, children_ref, index_in, weight_in, phase_in, table_in, out_ref,
    held_ref, left_ref, right_ref, index_ref, weight_ref, phase_ref, table_ref, lists_ref, spare_ref,
    high_ref, low_ref, high_a, low_a, fine_a, high_b, low_b, fine_b, outgoing_ref, grid_ref,
    counts_ref, sources_ref, summed_even, summed_odd, result_ref, landing_ref,
    load_sems, input_sems, self_sems, halo_send, halo_recv, list_send, list_recv,
    box_send, box_recv, dir_send, dir_recv, place_sems,
):
    tiles = held_ref.shape[0]
    chunks, boxes, _, _, block = grid_ref.shape
    dirs = lists_ref.shape[0]
    kinds = table_ref.shape[1]
    my_box, my_dir = lax.axis_index("box"), lax.axis_index("dir")
    first = my_dir * index_ref.shape[1]
    mesh_type = pl.DeviceIdType.MESH

    def dir_at(step):
        return (my_dir + step + dirs) % dirs

    def box_at(step):
        return (my_box + step + boxes) % boxes

    inputs = [
        pltpu.make_async_copy(source, target, input_sems.at[i])
        for i, (source, target) in enumerate(
            [
                (index_in, index_ref), (weight_in, weight_ref), (phase_in, phase_ref),
                (ids_in, lists_ref.at[my_dir, 0]), (kinds_in, lists_ref.at[my_dir, 1]),
                (lengths_in, spare_ref), (table_in.at[:, :, 0, my_dir], table_ref),
            ]
        )
    ]

    def load(tile):
        return pltpu.make_async_copy(
            children_ref.at[:, :, pl.ds(pl.multiple_of(tile * LANES, LANES), LANES)],
            held_ref.at[tile], load_sems.at[tile],
        )

    per = tiles // boxes
    early = (0, 1, 2) if chunks >= 3 else tuple(range(per))
    late = tuple(range(3, per)) if chunks >= 3 else ()

    def over_sections(offsets, act):
        @pl.loop(0, boxes)
        def _(section):
            for offset in offsets:
                act(section * per + offset)

    def prepare(tile):
        prepare_columns(held_ref, left_ref, right_ref, tile, high_ref, low_ref, parents)

    over_sections(early, lambda tile: load(tile).start())
    for copy in inputs[3:6] + inputs[:3]:
        copy.start()
    over_sections(late, lambda tile: load(tile).start())
    inputs[6].start()

    barrier = pltpu.get_barrier_semaphore()

    @pl.loop(1, dirs)
    def _(step):
        pl.semaphore_signal(barrier, inc=1, device_id={"dir": dir_at(step)}, device_id_type=mesh_type)

    @pl.loop(1, boxes)
    def _(step):
        pl.semaphore_signal(barrier, inc=1, device_id={"box": box_at(step)}, device_id_type=mesh_type)

    def clear():
        for ref in (high_a, low_a, high_b, low_b):
            ref[...] = jnp.zeros_like(ref)

    clear()
    over_sections(early, lambda tile: load(tile).wait())
    if chunks >= 3:
        over_sections((1, 2), prepare)
    else:

        @pl.loop(1, tiles)
        def _(tile):
            prepare(tile)

    pl.semaphore_wait(barrier, dirs + boxes - 2)

    halos = [
        pltpu.make_async_remote_copy(
            src_ref=children_ref.at[:, :, pl.ds(column, LANES)], dst_ref=target,
            send_sem=halo_send.at[i], recv_sem=halo_recv.at[i],
            device_id={"dir": dir_at(step)}, device_id_type=mesh_type,
        )
        for i, (column, target, step) in enumerate(
            [((tiles - 1) * LANES, left_ref, 1), (0, right_ref, -1)]
        )
    ]
    for copy in halos:
        copy.start()

    def list_copy(step, owner):
        return pltpu.make_async_remote_copy(
            src_ref=lists_ref.at[my_dir], dst_ref=lists_ref.at[owner],
            send_sem=list_send.at[step], recv_sem=list_recv.at[step],
            device_id={"dir": dir_at(step)}, device_id_type=mesh_type,
        )

    for copy in inputs[3:6]:
        copy.wait()
    square = (8, spare_ref.shape[1])
    own = lax.broadcasted_iota(jnp.int32, square, 0) == lax.broadcasted_iota(jnp.int32, square, 1)
    lengths = jnp.sum(jnp.where(own, spare_ref[...].astype(F32), 0.0), axis=1, keepdims=True)
    lists_ref[my_dir, 2] = jnp.broadcast_to(lengths, (8, lists_ref.shape[3])).astype(jnp.int32)

    @pl.loop(1, dirs)
    def _(step):
        list_copy(step, my_dir).start()

    def box_copy(chunk, step, owner):
        return pltpu.make_async_remote_copy(
            src_ref=outgoing_ref.at[chunk, step], dst_ref=grid_ref.at[chunk, owner],
            send_sem=box_send.at[chunk, step], recv_sem=box_recv.at[chunk, step],
            device_id={"box": box_at(step)}, device_id_type=mesh_type,
        )

    def own_box_copy(chunk):
        return pltpu.make_async_copy(
            outgoing_ref.at[chunk, 0], grid_ref.at[chunk, my_box], self_sems.at[0, chunk]
        )

    def dir_target(chunk, owner):
        return landing_ref.at[owner, :, :, pl.ds(pl.multiple_of(chunk * block, LANES), block)]

    def place(chunk, step):
        lanes = pl.ds(pl.multiple_of(chunk * block, LANES), block)
        return pltpu.make_async_copy(
            dir_target(chunk, dir_at(-step)), out_ref.at[:, :, 0, dir_at(-step), lanes],
            place_sems.at[chunk, step],
        )

    def dir_copy(chunk, step, owner):
        return pltpu.make_async_remote_copy(
            src_ref=result_ref.at[chunk, step], dst_ref=dir_target(chunk, owner),
            send_sem=dir_send.at[chunk, step], recv_sem=dir_recv.at[chunk, step],
            device_id={"dir": dir_at(step)}, device_id_type=mesh_type,
        )

    def own_dir_copy(chunk):
        return pltpu.make_async_copy(
            result_ref.at[chunk, 0], dir_target(chunk, my_dir), self_sems.at[1, chunk]
        )

    def rest():
        over_sections(late, lambda tile: load(tile).wait())
        over_sections(late, prepare)

        @pl.loop(1, boxes)
        def _(section):
            prepare(section * per)

    def edges():
        for copy in halos:
            copy.wait_recv()
        prepare_columns(held_ref, left_ref, right_ref, 0, high_ref, low_ref, parents)
        prepare_columns(held_ref, left_ref, right_ref, tiles, high_ref, low_ref, parents)

    def lists():
        @pl.loop(1, dirs)
        def _(step):
            list_copy(step, dir_at(-step)).wait_recv()

        count_pairs(lists_ref, kinds, sources_ref.shape[1] // 2, counts_ref)
        inputs[6].wait()

    for copy in inputs[:3]:
        copy.wait()

    def aggregate(chunk):
        @pl.loop(0, boxes // 2)
        def _(pair):
            steps = (2 * pair + 1, (2 * pair + 2) % boxes)
            if block != 512:
                clear()
            work = []
            for step, buffers in zip(steps, ((high_a, low_a, fine_a), (high_b, low_b, fine_b))):
                start = pl.multiple_of(box_at(step) * span + chunk * block, LANES)
                coarse = start // 4
                if block == 512:
                    base, shift = pl.multiple_of(coarse, LANES), 0
                else:
                    base = pl.multiple_of(coarse // LANES * LANES, LANES)
                    shift = coarse % LANES
                work.append((start, base, shift, step) + buffers)
            for start, base, shift, step, band_high, band_low, fine_ref in work:
                band_matrix(index_ref, weight_ref, start, first, shift, block, total, band_high, band_low)
            for start, base, shift, step, band_high, band_low, fine_ref in work:
                interpolate(high_ref, low_ref, base, band_high, band_low, fine_ref)
            for start, base, shift, step, band_high, band_low, fine_ref in work:
                rotate(phase_ref, start, fine_ref, parents, outgoing_ref.at[chunk, step])
            box_copy(chunk, steps[0], my_box).start()

            @pl.when(steps[1] > 0)
            def _():
                box_copy(chunk, steps[1], my_box).start()

        own_box_copy(chunk).start()

    def translate(chunk):
        own_box_copy(chunk).wait()

        @pl.loop(1, boxes)
        def _(step):
            box_copy(chunk, step, box_at(-step)).wait_recv()

        load_sources(grid_ref.at[chunk], sources_ref)
        count = sources_ref.shape[0]
        buffers = (summed_even, summed_odd)

        def sum_tile(d, tile, buffer):
            buffer[...] = jnp.dot(counts_ref[d], sources_ref[tile], preferred_element_type=F32)

        def step_at(turn):
            half = (turn + 1) // 2
            return (dirs // 2 + jnp.where(turn % 2 == 1, half, -half) + dirs) % dirs

        def items(step, following, parity):
            for tile in range(count):
                if tile + 1 < count:
                    sum_tile(dir_at(step), tile + 1, buffers[(parity + tile + 1) % 2])
                else:
                    sum_tile(dir_at(following), 0, buffers[(parity + tile + 1) % 2])
                multiply_tile(
                    buffers[(parity + tile) % 2], table_ref, chunk * block, tile, result_ref.at[chunk, step]
                )

        def send(step):
            @pl.when(step > 0)
            def _():
                dir_copy(chunk, step, my_dir).start()

        sum_tile(dir_at(step_at(0)), 0, summed_even)
        if count % 2 == 0:

            @pl.loop(0, dirs)
            def _(turn):
                step = step_at(turn)
                items(step, step_at(turn + 1), 0)
                send(step)

        else:

            @pl.loop(0, dirs // 2)
            def _(turn):
                for half in range(2):
                    step = step_at(2 * turn + half)
                    items(step, step_at(2 * turn + half + 1), half)
                    send(step)

        own_dir_copy(chunk).start()

    if chunks < 3:
        edges()

    @pl.loop(0, chunks + 1)
    def _(turn):
        if chunks >= 3:
            pl.when(turn == chunks - 2)(edges)

        @pl.when(turn < chunks)
        def _():
            aggregate((turn + 1) % chunks)

        @pl.when(turn == 0)
        def _():
            if chunks >= 3:
                rest()
            lists()

        @pl.when(turn > 0)
        def _():
            translate(turn % chunks)

    for copy in halos:
        copy.wait_send()

    @pl.loop(1, dirs)
    def _(step):
        list_copy(step, my_dir).wait_send()

    @pl.loop(0, chunks)
    def _(turn):
        chunk = (turn + 1) % chunks
        own_dir_copy(chunk).wait()
        place(chunk, 0).start()

        @pl.loop(1, dirs)
        def _(step):
            dir_copy(chunk, step, dir_at(-step)).wait_recv()
            place(chunk, step).start()

        @pl.loop(1, boxes)
        def _(step):
            box_copy(chunk, step, my_box).wait_send()

    @pl.loop(0, chunks)
    def _(chunk):
        @pl.loop(1, dirs)
        def _(step):
            dir_copy(chunk, step, my_dir).wait_send()

        @pl.loop(0, dirs)
        def _(step):
            place(chunk, step).wait()


def on_device(
    children, stencil_index, stencil_weights, child_phase, translations, box_lengths, partner_ids, partner_kinds
):
    boxes = lax.axis_size("box")
    dirs = lax.axis_size("dir")
    rows, coarse = children.shape[1:]
    fine = stencil_index.shape[1]
    parents = rows // 8
    span = fine // boxes
    kinds = translations.shape[1]
    sources = parents * boxes
    slots = partner_ids.shape[1]
    block, depth = block_layout(fine, span)
    chunks = span // block
    vmem, dma = pltpu.VMEM, pltpu.SemaphoreType.DMA
    return pl.pallas_call(
        functools.partial(fused_kernel, parents, span, coarse * dirs),
        out_shape=jax.ShapeDtypeStruct((2, 8, 1, dirs, span), F32),
        in_specs=[pl.BlockSpec(memory_space=pl.ANY)] * 8,
        out_specs=pl.BlockSpec(memory_space=pl.ANY),
        scratch_shapes=[
            vmem((coarse // LANES, 2, rows, LANES), F32),
            vmem((2, rows, LANES), F32),
            vmem((2, rows, LANES), F32),
            vmem(stencil_index.shape, jnp.int32),
            vmem(stencil_weights.shape, F32),
            vmem(child_phase.shape, F32),
            vmem((2, kinds, span), F32),
            vmem((dirs, 3, 8, slots), jnp.int32),
            vmem((1, box_lengths.shape[0]), jnp.int32),
            vmem((2 * rows, coarse + LANES), BF16),
            vmem((2 * rows, coarse + LANES), BF16),
            vmem((depth, block), BF16),
            vmem((depth, block), BF16),
            vmem((2 * rows, block), F32),
            vmem((depth, block), BF16),
            vmem((depth, block), BF16),
            vmem((2 * rows, block), F32),
            vmem((chunks, boxes, 2, parents, block), F32),
            vmem((chunks, boxes, 2, parents, block), F32),
            vmem((dirs, kinds * 8, 2 * sources), BF16),
            vmem((block // LANES, 2 * sources, 2 * LANES), BF16),
            vmem((kinds * 8, 2 * LANES), F32),
            vmem((kinds * 8, 2 * LANES), F32),
            vmem((chunks, dirs, 2, 8, block), F32),
            vmem((dirs, 2, 8, span), F32),
            dma((coarse // LANES,)),
            dma((7,)),
            dma((2, chunks)),
            dma((2,)),
            dma((2,)),
            dma((dirs,)),
            dma((dirs,)),
            dma((chunks, boxes)),
            dma((chunks, boxes)),
            dma((chunks, dirs)),
            dma((chunks, dirs)),
            dma((chunks, dirs)),
        ],
        compiler_params=pltpu.CompilerParams(
            collective_id=0, has_side_effects=True, vmem_limit_bytes=56 << 20
        ),
    )(partner_ids, partner_kinds, box_lengths.reshape(1, -1), children, stencil_index, stencil_weights, child_phase, translations)


def solution(mesh):
    return jax.shard_map(
        on_device,
        mesh=mesh,
        in_specs=(
            P(None, "box", "dir"),
            P(None, "dir"),
            P(None, "dir"),
            P(None, "dir"),
            P(None, None, "box", None, None),
            P("dir"),
            P("dir", None),
            P("dir", None),
        ),
        out_specs=P(None, "dir", "box", None, None),
        check_vma=False,
    )
```
